128 devices in a mesh: row: 8 (over z, core), col: 16 (over y, x).
Axes of the slice: x: 4, y: 4, z: 4, core: 2. Of those that a mesh axis runs over, the one named last changes fastest.
Arguments:
- tokens: bfloat16 [768, 10240], P('row', 'col'), may hold values from -6 to 6
- weight: bfloat16 [10240, 40960], P('col', 'row'), may hold values from -0.0625 to 0.0625
- upstream: bfloat16 [768, 40960], P('col', 'row'), may hold values from -6 to 6
Outputs:
- grad_input: bfloat16 [768, 10240], P('row', 'col')
- grad_weight: bfloat16 [10240, 40960], P('col', 'row')
The draws below stay inside these ranges and needn't reach their ends.
All inputs are finite; a program needn't handle non-finite values.
Results may differ from the reference program's by a relative error of at most 0.0049.
Values may be sent and summed in bfloat16 or wider, within the bound.
A program may use at most 128 MiB of HBM per device.

```python
import jax
import jax.numpy as jnp

D = 10240
F = 40960
TOKENS = 768


def steps_of(stream_key, dims, cuts, low, high):
    factor_of, own = 1.0, jax.random.fold_in(stream_key, 6)
    for axis_at, shards_of in cuts:
        steps = jnp.exp(jax.random.uniform(jax.random.fold_in(own, axis_at), (shards_of,), jnp.float32, low / len(cuts), high / len(cuts)))
        factor_of = factor_of * jnp.repeat(steps, dims[axis_at] // shards_of).reshape([-1 if axis == axis_at else 1 for axis in range(len(dims))])
    return factor_of


def bell_draw(stream_key, extent, spread, bound, shards=(), kind=jnp.bfloat16):
    drawn = spread * jax.random.normal(stream_key, extent, jnp.float32)
    if shards:
        drawn = drawn * steps_of(stream_key, extent, shards, -0.22, 0.18)
    return jnp.clip(drawn, -bound, bound).astype(kind)


def setup_inputs(seed: int = 0) -> dict:
    streams_of = jax.random.split(jax.random.key(seed), 4)
    tokens = bell_draw(streams_of[0], (TOKENS, D), 1.0, 6.0, ((0, 8), (1, 16)))
    weight = bell_draw(streams_of[1], (D, F), D ** -0.5, 0.0625, ((0, 16), (1, 8)))
    upstream = bell_draw(streams_of[2], (TOKENS, F), 1.0, 6.0, ((0, 16), (1, 8)))
    return dict(tokens=tokens, weight=weight, upstream=upstream)


def gelu_slope(value):
    coeff = 0.7978845608028654
    inner = coeff * (value + 0.044715 * value * value * value)
    tanh_value = jnp.tanh(inner)
    return 0.5 * (1.0 + tanh_value) + 0.5 * value * (1.0 - tanh_value * tanh_value) * coeff * (1.0 + 3.0 * 0.044715 * value * value)


def reference(tokens, weight, upstream):
    pre = jnp.dot(tokens, weight, preferred_element_type=jnp.float32)
    grad_pre = (upstream.astype(jnp.float32) * gelu_slope(pre)).astype(jnp.bfloat16)
    grad_input = jnp.dot(grad_pre, weight.T, preferred_element_type=jnp.float32).astype(jnp.bfloat16)
    grad_weight = jnp.dot(tokens.T, grad_pre, preferred_element_type=jnp.float32).astype(jnp.bfloat16)
    return grad_input, grad_weight
```

```python
import functools

import jax
import jax.numpy as jnp
from jax import lax
from jax.experimental import pallas as pl
from jax.experimental.pallas import tpu as pltpu
from jax.sharding import PartitionSpec

N_CHUNKS = 10
BF16 = jnp.bfloat16
F32 = jnp.float32
MESH = pl.DeviceIdType.MESH


def gelu_slope(value):
    coeff = 0.7978845608028654
    inner = coeff * (value + 0.044715 * value * value * value)
    tanh_value = jnp.tanh(inner)
    return 0.5 * (1.0 + tanh_value) + 0.5 * value * (1.0 - tanh_value * tanh_value) * coeff * (
        1.0 + 3.0 * 0.044715 * value * value
    )


def mod4(value):
    return lax.rem(value + 4, 4)


def kernel(
    n, part, slab,
    tin, w_hbm, up, gi_out, gw_hbm,
    tok, tok_t, wv, pf, snd1, rcv1, sndc, rcvc, s2, snd2, rcv2, snd2c, rcv2c, g, giacc, gws,
    gx, gt, zs1, zr1, zsc, zrc,
    ssem, rsem, tsem_s, tsem_r, xsem_s, xsem_r, wsem, osem, lsem,
):
    row, col = lax.axis_index("row"), lax.axis_index("col")
    z, core = lax.div(row, 2), lax.rem(row, 2)
    y, x = lax.div(col, 4), lax.rem(col, 4)
    half = part // 2

    def x_dev(d):
        return {"col": y * 4 + mod4(x + d)}

    def y_dev(d):
        return {"col": mod4(y + d) * 4 + x}

    def z_dev(d):
        return {"row": mod4(z + d) * 2 + core}

    sib_dev = {"row": z * 2 + (1 - core)}
    sign = (1, -1)
    major, minor = (x, y), (y, x)
    major_dev, minor_dev = (x_dev, y_dev), (y_dev, x_dev)

    def at(s, m, k):
        return (k, m) if s == 0 else (m, k)

    def w_copy(c):
        return pltpu.make_async_copy(
            w_hbm.at[:, pl.ds(pl.multiple_of(c * 2 * part, 2 * part), 2 * part)], wv.at[c], wsem.at[c]
        )

    for c in range(n):
        w_copy(c).start()
    own_tok = pltpu.make_async_copy(tin, tok.at[z, core], lsem)
    own_tok.start()

    barrier = pltpu.get_barrier_semaphore()
    for dev in (x_dev(1), x_dev(-1), y_dev(1), y_dev(-1), z_dev(1), z_dev(-1), sib_dev):
        pl.semaphore_signal(barrier, inc=1, device_id=dev, device_id_type=MESH)
    pl.semaphore_wait(barrier, 7)

    def t_copy(src, dst, which, dev):
        return pltpu.make_async_remote_copy(
            src_ref=src, dst_ref=dst, send_sem=tsem_s.at[which], recv_sem=tsem_r.at[which],
            device_id=dev, device_id_type=MESH,
        )

    def t_region(which):
        return {
            0: lambda zz, cc: tok.at[zz, cc],
            1: lambda zz, cc: tok.at[zz, cc, 0],
            2: lambda zz, cc: tok.at[zz, cc, 1],
        }[which]

    zm, zp, zo = mod4(z - 1), mod4(z + 1), mod4(z + 2)
    full, lo, hi = t_region(0), t_region(1), t_region(2)
    sends = [
        t_copy(tin, full(z, core), 0, z_dev(1)),
        t_copy(tin, full(z, core), 1, z_dev(-1)),
        t_copy(tin, full(z, core), 2, sib_dev),
    ]
    for cp in sends:
        cp.start()

    def t_wait(region, which):
        t_copy(region, region, which, sib_dev).wait_recv()

    def t_send(region, which, dev):
        cp = t_copy(region, region, which, dev)
        cp.start()
        sends.append(cp)

    t_wait(full(zm, core), 0)
    t_send(lo(zm, core), 3, z_dev(1))
    t_send(full(zm, core), 5, sib_dev)
    t_wait(full(zp, core), 1)
    t_send(hi(zp, core), 4, z_dev(-1))
    t_send(full(zp, core), 6, sib_dev)
    t_wait(lo(zo, core), 3)
    t_send(lo(zo, core), 7, sib_dev)
    t_wait(hi(zo, core), 4)
    t_send(hi(zo, core), 8, sib_dev)
    other = 1 - core
    t_wait(full(z, other), 2)
    t_wait(full(zm, other), 5)
    t_wait(full(zp, other), 6)
    t_wait(lo(zo, other), 7)
    t_wait(hi(zo, other), 8)
    own_tok.wait()

    tokens_all = 16 * slab

    def r_copy(src, dst, kind, c, s, d, dev):
        return pltpu.make_async_remote_copy(
            src_ref=src, dst_ref=dst, send_sem=ssem.at[c, s, kind, d], recv_sem=rsem.at[c, s, kind, d],
            device_id=dev, device_id_type=MESH,
        )

    def r_wait(region, kind, c, s, d):
        r_copy(region, region, kind, c, s, d, sib_dev).wait_recv()

    def s_wait(region, kind, c, s, d):
        r_copy(region, region, kind, c, s, d, sib_dev).wait_send()

    def cols_of(s):
        return slice(s * part, (s + 1) * part)

    def stage0(c):
        slot = lax.rem(c, 3)
        w_copy(c).wait()
        out = jnp.dot(
            tok[...].reshape(tokens_all, tok.shape[-1]), wv[c], preferred_element_type=F32
        )
        pf[slot] = out.reshape(4, 4, slab, 2 * part)
        for s in (0, 1):
            m, cols = major[s], cols_of(s)
            for j in (0, 1):
                def piece(mm, k):
                    a, b = at(s, mm, k)
                    return pf[slot, a, b, :, cols].astype(BF16)

                snd1[c, s, 0, 0, j] = piece(mod4(m + 2), j)
                snd1[c, s, 0, 1, j] = piece(mod4(m + 1), 2 + j)
                snd1[c, s, 1, 0, j] = piece(mod4(m + 2), 2 + j)
                snd1[c, s, 1, 1, j] = piece(mod4(m - 1), j)
            for d in (0, 1):
                r_copy(snd1.at[c, s, d], rcv1.at[c, s, d], 0, c, s, d, major_dev[s](sign[d])).start()

    def stage1(c):
        slot = lax.rem(c, 3)
        for s in (0, 1):
            m, cols = major[s], cols_of(s)
            for d in (0, 1):
                r_wait(rcv1.at[c, s, d], 0, c, s, d)
                for j in (0, 1):
                    a, b = at(s, mod4(m + sign[d]), 2 * d + j)
                    sndc[c, s, d, j] = (
                        pf[slot, a, b, :, cols] + rcv1[c, s, d, 0, j].astype(F32)
                    ).astype(BF16)
                r_copy(sndc.at[c, s, d], rcvc.at[c, s, d], 1, c, s, d, major_dev[s](sign[d])).start()

    def stage2(c):
        slot = lax.rem(c, 3)
        for s in (0, 1):
            m, k, cols = major[s], minor[s], cols_of(s)
            for d in (0, 1):
                r_wait(rcvc.at[c, s, d], 1, c, s, d)
            for kk in range(4):
                a, b = at(s, m, kk)
                h, j = kk // 2, kk % 2
                s2[slot, s, kk] = (
                    pf[slot, a, b, :, cols]
                    + rcvc[c, s, h, j].astype(F32)
                    + rcv1[c, s, 1 - h, 1, j].astype(F32)
                )
            lo_c, hi_c = slice(0, half), slice(half, part)
            snd2[c, s, 0, 0] = s2[slot, s, mod4(k + 2), :, lo_c].astype(BF16)
            snd2[c, s, 0, 1] = s2[slot, s, mod4(k + 1), :, hi_c].astype(BF16)
            snd2[c, s, 1, 0] = s2[slot, s, mod4(k + 2), :, hi_c].astype(BF16)
            snd2[c, s, 1, 1] = s2[slot, s, mod4(k - 1), :, lo_c].astype(BF16)
            for d in (0, 1):
                r_copy(snd2.at[c, s, d], rcv2.at[c, s, d], 2, c, s, d, minor_dev[s](sign[d])).start()

    def stage3(c):
        slot = lax.rem(c, 3)
        for s in (0, 1):
            k = minor[s]
            for d in (0, 1):
                r_wait(rcv2.at[c, s, d], 2, c, s, d)
                cols = slice(d * half, (d + 1) * half)
                snd2c[c, s, d] = (
                    s2[slot, s, mod4(k + sign[d]), :, cols] + rcv2[c, s, d, 0].astype(F32)
                ).astype(BF16)
                r_copy(snd2c.at[c, s, d], rcv2c.at[c, s, d], 3, c, s, d, minor_dev[s](sign[d])).start()

    def stage4(c):
        slot = lax.rem(c, 3)
        for s in (0, 1):
            m, k = major[s], minor[s]
            a, b = at(s, m, k)
            for d in (0, 1):
                r_wait(rcv2c.at[c, s, d], 3, c, s, d)
            for h in (0, 1):
                cols = slice(h * half, (h + 1) * half)
                pre = (
                    s2[slot, s, k, :, cols]
                    + rcv2c[c, s, h].astype(F32)
                    + rcv2[c, s, 1 - h, 1].astype(F32)
                )
                at_col = pl.multiple_of(c * 2 * part + s * part + h * half, half)
                upstream = up[:, pl.ds(at_col, half)].astype(F32)
                g[c, s, a, b, :, cols] = (upstream * gelu_slope(pre)).astype(BF16)
            own = g.at[c, s, a, b]
            for d in (0, 1):
                r_copy(own, own, 4, c, s, d, minor_dev[s](sign[d])).start()

    def near(c, s, d):
        a, b = at(s, major[s], mod4(minor[s] - sign[d]))
        return g.at[c, s, a, b], g.at[c, s, a, b, :, pl.ds(d * half, half)]

    def far(c, s, d):
        a, b = at(s, major[s], mod4(minor[s] + 2))
        return g.at[c, s, a, b, :, pl.ds(d * half, half)]

    def stage5(c):
        for s in (0, 1):
            for d in (0, 1):
                whole, onward = near(c, s, d)
                r_wait(whole, 4, c, s, d)
                r_copy(onward, onward, 5, c, s, d, minor_dev[s](sign[d])).start()

    def line(c, s, m):
        return g.at[c, s, :, m] if s == 0 else g.at[c, s, m]

    def half_line(c, s, m, d):
        return g.at[c, s, pl.ds(2 * d, 2), m] if s == 0 else g.at[c, s, m, pl.ds(2 * d, 2)]

    def stage6(c):
        for s in (0, 1):
            for d in (0, 1):
                r_wait(far(c, s, d), 5, c, s, d)
            own = line(c, s, major[s])
            for d in (0, 1):
                r_copy(own, own, 6, c, s, d, major_dev[s](sign[d])).start()

    def stage7(c):
        for s in (0, 1):
            for d in (0, 1):
                m = mod4(major[s] - sign[d])
                r_wait(line(c, s, m), 6, c, s, d)
                onward = half_line(c, s, m, d)
                r_copy(onward, onward, 7, c, s, d, major_dev[s](sign[d])).start()

    def o_copy(c):
        slot = lax.rem(c, 2)
        return pltpu.make_async_copy(
            gws.at[slot],
            gw_hbm.at[:, pl.ds(pl.multiple_of(c * 2 * part, 2 * part), 2 * part)],
            osem.at[slot],
        )

    def grad_of(c, s):
        return g[c, s].reshape(tokens_all, part)

    def land(c):
        for s in (0, 1):
            for d in (0, 1):
                r_wait(half_line(c, s, mod4(major[s] + 2), d), 7, c, s, d)

    def input_grad(c):
        total = None
        for s in (0, 1):
            term = lax.dot_general(
                grad_of(c, s), wv[c, :, cols_of(s)], (((1,), (1,)), ((), ())), preferred_element_type=F32
            )
            total = term if total is None else total + term
        giacc[...] += total.reshape(giacc.shape)

    def weight_grad(c):
        slot = lax.rem(c, 2)
        for s in (0, 1):
            gws[slot, :, cols_of(s)] = jnp.dot(
                tok_t[...], grad_of(c, s), preferred_element_type=F32
            ).astype(BF16)
        o_copy(c).start()

    def settle(c):
        for s in (0, 1):
            m, k = major[s], minor[s]
            a, b = at(s, m, k)
            for d in (0, 1):
                s_wait(snd1.at[c, s, d], 0, c, s, d)
                s_wait(sndc.at[c, s, d], 1, c, s, d)
                s_wait(snd2.at[c, s, d], 2, c, s, d)
                s_wait(snd2c.at[c, s, d], 3, c, s, d)
                s_wait(g.at[c, s, a, b], 4, c, s, d)
                s_wait(near(c, s, d)[1], 5, c, s, d)
                s_wait(line(c, s, m), 6, c, s, d)
                s_wait(half_line(c, s, mod4(m - sign[d]), d), 7, c, s, d)

    def stage8(c):
        land(c)
        input_grad(c)

        @pl.when(c >= 2)
        def _():
            o_copy(c - 2).wait()

        weight_grad(c)
        settle(c)

    @pl.loop(0, n + 7)
    def _(i):
        for offset, stage in enumerate(
            (stage0, stage1, stage2, stage3, stage4, stage5, stage6, stage7)
        ):
            @pl.when((i >= offset) & (i < n + offset))
            def _(offset=offset, stage=stage):
                stage(i - offset)

            if offset == 0:
                @pl.when(i == 5)
                def _():
                    for cp in sends:
                        cp.wait_send()
                    giacc[...] = jnp.zeros_like(giacc)
                    tok_t[...] = tok[...].reshape(tokens_all, tok.shape[-1]).T

        @pl.when((i >= 8))
        def _():
            stage8(i - 8)

    last = n - 1
    land(last)
    input_grad(last)

    def x_copy(src, dst, which, dev):
        return pltpu.make_async_remote_copy(
            src_ref=src, dst_ref=dst, send_sem=xsem_s.at[which], recv_sem=xsem_r.at[which],
            device_id=dev, device_id_type=MESH,
        )

    cross = x_copy(giacc.at[:, other], gx, 0, sib_dev)
    cross.start()
    o_copy(last - 2).wait()
    weight_grad(last)
    settle(last)
    cross.wait()
    gt[...] = giacc[:, core] + gx[...]
    wire = zs1.dtype
    zs1[0, 0] = gt[zo, 0].astype(wire)
    zs1[0, 1] = gt[zp, 1].astype(wire)
    zs1[1, 0] = gt[zo, 1].astype(wire)
    zs1[1, 1] = gt[zm, 0].astype(wire)
    first = [x_copy(zs1.at[d], zr1.at[d], 1 + d, z_dev(sign[d])) for d in (0, 1)]
    for cp in first:
        cp.start()
    second = []
    for d in (0, 1):
        first[d].wait()
        zsc[d] = (gt[mod4(z + sign[d]), d] + zr1[d, 0].astype(F32)).astype(wire)
        cp = x_copy(zsc.at[d], zrc.at[d], 3 + d, z_dev(sign[d]))
        cp.start()
        second.append(cp)
    for cp in second:
        cp.wait()
    for h in (0, 1):
        gi_out[pl.ds(h * slab, slab), :] = (
            gt[z, h] + zrc[h].astype(F32) + zr1[1 - h, 1].astype(F32)
        ).astype(BF16)
    o_copy(last - 1).wait()
    o_copy(last).wait()


def local(tokens, weight, upstream):
    rows, depth = tokens.shape
    width = weight.shape[1]
    slab = upstream.shape[0]
    n = N_CHUNKS
    part = width // (2 * n)
    half = part // 2
    wire = BF16
    vmem, dma = pltpu.VMEM, pltpu.SemaphoreType.DMA
    scratch = [
        vmem((4, 2, 2, slab, depth), BF16),
        vmem((depth, 16 * slab), BF16),
        vmem((n, depth, 2 * part), BF16),
        vmem((3, 4, 4, slab, 2 * part), F32),
        vmem((n, 2, 2, 2, 2, slab, part), BF16),
        vmem((n, 2, 2, 2, 2, slab, part), BF16),
        vmem((n, 2, 2, 2, slab, part), BF16),
        vmem((n, 2, 2, 2, slab, part), BF16),
        vmem((3, 2, 4, slab, part), F32),
        vmem((n, 2, 2, 2, slab, half), BF16),
        vmem((n, 2, 2, 2, slab, half), BF16),
        vmem((n, 2, 2, slab, half), BF16),
        vmem((n, 2, 2, slab, half), BF16),
        vmem((n, 2, 4, 4, slab, part), BF16),
        vmem((4, 2, 2, slab, depth), F32),
        vmem((2, depth, 2 * part), BF16),
        vmem((4, 2, slab, depth), F32),
        vmem((4, 2, slab, depth), F32),
        vmem((2, 2, slab, depth), wire),
        vmem((2, 2, slab, depth), wire),
        vmem((2, slab, depth), wire),
        vmem((2, slab, depth), wire),
        dma((n, 2, 8, 2)),
        dma((n, 2, 8, 2)),
        dma((9,)),
        dma((9,)),
        dma((5,)),
        dma((5,)),
        dma((n,)),
        dma((2,)),
        dma,
    ]
    return pl.pallas_call(
        functools.partial(kernel, n, part, slab),
        out_shape=(
            jax.ShapeDtypeStruct((rows, depth), BF16),
            jax.ShapeDtypeStruct((depth, width), BF16),
        ),
        in_specs=[
            pl.BlockSpec(memory_space=pltpu.VMEM),
            pl.BlockSpec(memory_space=pl.ANY),
            pl.BlockSpec(memory_space=pltpu.VMEM),
        ],
        out_specs=(
            pl.BlockSpec(memory_space=pltpu.VMEM),
            pl.BlockSpec(memory_space=pl.ANY),
        ),
        scratch_shapes=scratch,
        compiler_params=pltpu.CompilerParams(
            collective_id=0, has_side_effects=True, vmem_limit_bytes=60 * 1024 * 1024
        ),
        cost_estimate=pl.CostEstimate(
            flops=6 * 16 * slab * depth * width, bytes_accessed=4 * depth * width, transcendentals=slab * width
        ),
    )(tokens.reshape(2, rows // 2, depth), weight, upstream)


def solution(mesh):
    spec = PartitionSpec
    return jax.shard_map(
        local,
        mesh=mesh,
        in_specs=(spec("row", "col"), spec("col", "row"), spec("col", "row")),
        out_specs=(spec("row", "col"), spec("col", "row")),
        check_vma=False,
    )
```

```python
import functools

import jax
import jax.numpy as jnp
from jax import lax
from jax.experimental import pallas as pl
from jax.experimental.pallas import tpu as pltpu
from jax.sharding import PartitionSpec

N_CHUNKS = 5
BF16 = jnp.bfloat16
F32 = jnp.float32
MESH = pl.DeviceIdType.MESH


def gelu_slope(value):
    coeff = 0.7978845608028654
    inner = coeff * (value + 0.044715 * value * value * value)
    tanh_value = jnp.tanh(inner)
    return 0.5 * (1.0 + tanh_value) + 0.5 * value * (1.0 - tanh_value * tanh_value) * coeff * (
        1.0 + 3.0 * 0.044715 * value * value
    )


def mod4(value):
    return lax.rem(value + 4, 4)


def kernel(
    n, part, slab,
    tin, w_hbm, up_hbm, gi_out, gw_out,
    up, tok, tok_t, wv, pf, snd1, rcv1, sndc, rcvc, s2, snd2, rcv2, snd2c, rcv2c, g, giacc,
    gx, zs1, zr1, zsc, zrc,
    ssem, rsem, tsem_s, tsem_r, xsem_s, xsem_r, wsem, lsem,
):
    row, col = lax.axis_index("row"), lax.axis_index("col")
    z, core = lax.div(row, 2), lax.rem(row, 2)
    y, x = lax.div(col, 4), lax.rem(col, 4)
    half = part // 2

    def x_dev(d):
        return {"col": y * 4 + mod4(x + d)}

    def y_dev(d):
        return {"col": mod4(y + d) * 4 + x}

    def z_dev(d):
        return {"row": mod4(z + d) * 2 + core}

    sib_dev = {"row": z * 2 + (1 - core)}
    sign = (1, -1)
    major, minor = (x, y), (y, x)
    major_dev, minor_dev = (x_dev, y_dev), (y_dev, x_dev)

    def at(s, m, k):
        return (k, m) if s == 0 else (m, k)

    def w_copy(c):
        return pltpu.make_async_copy(
            w_hbm.at[:, pl.ds(pl.multiple_of(c * 2 * part, 2 * part), 2 * part)], wv.at[c], wsem.at[c]
        )

    barrier = pltpu.get_barrier_semaphore()
    for dev in (x_dev(1), x_dev(-1), y_dev(1), y_dev(-1), z_dev(1), z_dev(-1), sib_dev):
        pl.semaphore_signal(barrier, inc=1, device_id=dev, device_id_type=MESH)
    own_tok = pltpu.make_async_copy(tin, tok.at[z, core], lsem.at[0])
    own_tok.start()
    for c in range(n):
        w_copy(c).start()
    own_up = pltpu.make_async_copy(up_hbm, up, lsem.at[1])
    own_up.start()
    own_tok.wait()
    pl.semaphore_wait(barrier, 7)

    def t_copy(region, which, dev):
        return pltpu.make_async_remote_copy(
            src_ref=region, dst_ref=region, send_sem=tsem_s.at[which], recv_sem=tsem_r.at[which],
            device_id=dev, device_id_type=MESH,
        )

    def full(zz, cc):
        return tok.at[zz, cc]

    def lo(zz, cc):
        return tok.at[zz, cc, 0]

    def hi(zz, cc):
        return tok.at[zz, cc, 1]

    zm, zp, zo = mod4(z - 1), mod4(z + 1), mod4(z + 2)
    other = 1 - core
    tokens_all = 16 * slab
    sends = []

    def t_send(region, which, dev):
        cp = t_copy(region, which, dev)
        cp.start()
        sends.append(cp)

    def t_wait(region, which):
        t_copy(region, which, sib_dev).wait_recv()

    def first_pre(zz):
        rows = tok[zz].reshape(4 * slab, tok.shape[-1])
        pf[0, zz] = jnp.dot(rows, wv[0], preferred_element_type=F32).reshape(4, slab, 2 * part)

    t_send(lo(z, core), 0, z_dev(1))
    t_send(hi(z, core), 2, z_dev(-1))
    t_send(hi(z, core), 1, z_dev(1))
    t_send(lo(z, core), 3, z_dev(-1))
    t_send(full(z, core), 4, sib_dev)
    w_copy(0).wait()
    t_wait(full(z, other), 4)
    t_wait(lo(zm, core), 0)
    t_send(lo(zm, core), 5, z_dev(1))
    t_wait(hi(zp, core), 2)
    t_send(hi(zp, core), 6, z_dev(-1))
    first_pre(z)
    t_wait(hi(zm, core), 1)
    t_send(full(zm, core), 7, sib_dev)
    t_wait(lo(zp, core), 3)
    t_send(full(zp, core), 8, sib_dev)
    t_wait(full(zm, other), 7)
    first_pre(zm)
    t_wait(lo(zo, core), 5)
    t_send(lo(zo, core), 9, sib_dev)
    t_wait(hi(zo, core), 6)
    t_send(hi(zo, core), 10, sib_dev)
    t_wait(full(zp, other), 8)
    first_pre(zp)
    t_wait(lo(zo, other), 9)
    t_wait(hi(zo, other), 10)
    first_pre(zo)
    own_up.wait()


    def r_copy(src, dst, kind, c, s, d, dev):
        return pltpu.make_async_remote_copy(
            src_ref=src, dst_ref=dst, send_sem=ssem.at[c, s, kind, d], recv_sem=rsem.at[c, s, kind, d],
            device_id=dev, device_id_type=MESH,
        )

    def r_wait(region, kind, c, s, d):
        r_copy(region, region, kind, c, s, d, sib_dev).wait_recv()

    def s_wait(region, kind, c, s, d):
        r_copy(region, region, kind, c, s, d, sib_dev).wait_send()

    def cols_of(s):
        return slice(s * part, (s + 1) * part)

    def stage0(c):
        slot = lax.rem(c, 3)

        @pl.when(c > 0)
        def _():
            w_copy(c).wait()
            out = jnp.dot(
                tok[...].reshape(tokens_all, tok.shape[-1]), wv[c], preferred_element_type=F32
            )
            pf[slot] = out.reshape(4, 4, slab, 2 * part)

        for s in (0, 1):
            m, cols = major[s], cols_of(s)
            for j in (0, 1):
                def piece(mm, k):
                    a, b = at(s, mm, k)
                    return pf[slot, a, b, :, cols].astype(BF16)

                snd1[c, s, 0, 0, j] = piece(mod4(m + 2), j)
                snd1[c, s, 0, 1, j] = piece(mod4(m + 1), 2 + j)
                snd1[c, s, 1, 0, j] = piece(mod4(m + 2), 2 + j)
                snd1[c, s, 1, 1, j] = piece(mod4(m - 1), j)
            for d in (0, 1):
                r_copy(snd1.at[c, s, d], rcv1.at[c, s, d], 0, c, s, d, major_dev[s](sign[d])).start()

    def stage1(c):
        slot = lax.rem(c, 3)
        for s in (0, 1):
            m, cols = major[s], cols_of(s)
            for d in (0, 1):
                r_wait(rcv1.at[c, s, d], 0, c, s, d)
                for j in (0, 1):
                    a, b = at(s, mod4(m + sign[d]), 2 * d + j)
                    sndc[c, s, d, j] = (
                        pf[slot, a, b, :, cols] + rcv1[c, s, d, 0, j].astype(F32)
                    ).astype(BF16)
                r_copy(sndc.at[c, s, d], rcvc.at[c, s, d], 1, c, s, d, major_dev[s](sign[d])).start()

    def stage2(c):
        slot = lax.rem(c, 3)
        for s in (0, 1):
            m, k, cols = major[s], minor[s], cols_of(s)
            for d in (0, 1):
                r_wait(rcvc.at[c, s, d], 1, c, s, d)
            for kk in range(4):
                a, b = at(s, m, kk)
                h, j = kk // 2, kk % 2
                s2[slot, s, kk] = (
                    pf[slot, a, b, :, cols]
                    + rcvc[c, s, h, j].astype(F32)
                    + rcv1[c, s, 1 - h, 1, j].astype(F32)
                )
            lo_c, hi_c = slice(0, half), slice(half, part)
            snd2[c, s, 0, 0] = s2[slot, s, mod4(k + 2), :, lo_c].astype(BF16)
            snd2[c, s, 0, 1] = s2[slot, s, mod4(k + 1), :, hi_c].astype(BF16)
            snd2[c, s, 1, 0] = s2[slot, s, mod4(k + 2), :, hi_c].astype(BF16)
            snd2[c, s, 1, 1] = s2[slot, s, mod4(k - 1), :, lo_c].astype(BF16)
            for d in (0, 1):
                r_copy(snd2.at[c, s, d], rcv2.at[c, s, d], 2, c, s, d, minor_dev[s](sign[d])).start()

    def stage3(c):
        slot = lax.rem(c, 3)
        for s in (0, 1):
            k = minor[s]
            for d in (0, 1):
                r_wait(rcv2.at[c, s, d], 2, c, s, d)
                cols = slice(d * half, (d + 1) * half)
                snd2c[c, s, d] = (
                    s2[slot, s, mod4(k + sign[d]), :, cols] + rcv2[c, s, d, 0].astype(F32)
                ).astype(BF16)
                r_copy(snd2c.at[c, s, d], rcv2c.at[c, s, d], 3, c, s, d, minor_dev[s](sign[d])).start()

    def stage4(c):
        slot = lax.rem(c, 3)
        for s in (0, 1):
            m, k = major[s], minor[s]
            a, b = at(s, m, k)
            for d in (0, 1):
                r_wait(rcv2c.at[c, s, d], 3, c, s, d)
            for h in (0, 1):
                cols = slice(h * half, (h + 1) * half)
                pre = (
                    s2[slot, s, k, :, cols]
                    + rcv2c[c, s, h].astype(F32)
                    + rcv2[c, s, 1 - h, 1].astype(F32)
                )
                at_col = pl.multiple_of(c * 2 * part + s * part + h * half, half)
                upstream = up[:, pl.ds(at_col, half)].astype(F32)
                g[c, s, a, b, :, cols] = (upstream * gelu_slope(pre)).astype(BF16)
            own = g.at[c, s, a, b]
            for d in (0, 1):
                r_copy(own, own, 4, c, s, d, minor_dev[s](sign[d])).start()

    def near(c, s, d):
        a, b = at(s, major[s], mod4(minor[s] - sign[d]))
        return g.at[c, s, a, b], g.at[c, s, a, b, :, pl.ds(d * half, half)]

    def far(c, s, d):
        a, b = at(s, major[s], mod4(minor[s] + 2))
        return g.at[c, s, a, b, :, pl.ds(d * half, half)]

    def stage5(c):
        for s in (0, 1):
            for d in (0, 1):
                whole, onward = near(c, s, d)
                r_wait(whole, 4, c, s, d)
                r_copy(onward, onward, 5, c, s, d, minor_dev[s](sign[d])).start()

    def line(c, s, m):
        return g.at[c, s, :, m] if s == 0 else g.at[c, s, m]

    def half_line(c, s, m, d):
        return g.at[c, s, pl.ds(2 * d, 2), m] if s == 0 else g.at[c, s, m, pl.ds(2 * d, 2)]

    def stage6(c):
        for s in (0, 1):
            for d in (0, 1):
                r_wait(far(c, s, d), 5, c, s, d)
            own = line(c, s, major[s])
            for d in (0, 1):
                r_copy(own, own, 6, c, s, d, major_dev[s](sign[d])).start()

    def stage7(c):
        for s in (0, 1):
            for d in (0, 1):
                m = mod4(major[s] - sign[d])
                r_wait(line(c, s, m), 6, c, s, d)
                onward = half_line(c, s, m, d)
                r_copy(onward, onward, 7, c, s, d, major_dev[s](sign[d])).start()

    def grad_of(c, s):
        return g[c, s].reshape(tokens_all, part)

    def land(c):
        for s in (0, 1):
            for d in (0, 1):
                r_wait(half_line(c, s, mod4(major[s] + 2), d), 7, c, s, d)

    def input_grad(c):
        total = None
        for s in (0, 1):
            term = lax.dot_general(
                grad_of(c, s), wv[c, :, cols_of(s)], (((1,), (1,)), ((), ())), preferred_element_type=F32
            )
            total = term if total is None else total + term
        giacc[...] += total.reshape(giacc.shape)

    def weight_grad(c):
        for s in (0, 1):
            gw_out[:, pl.ds(pl.multiple_of((c * 2 + s) * part, part), part)] = jnp.dot(
                tok_t[...], grad_of(c, s), preferred_element_type=F32
            ).astype(BF16)

    def settle(c):
        for s in (0, 1):
            m, k = major[s], minor[s]
            a, b = at(s, m, k)
            for d in (0, 1):
                s_wait(snd1.at[c, s, d], 0, c, s, d)
                s_wait(sndc.at[c, s, d], 1, c, s, d)
                s_wait(snd2.at[c, s, d], 2, c, s, d)
                s_wait(snd2c.at[c, s, d], 3, c, s, d)
                s_wait(g.at[c, s, a, b], 4, c, s, d)
                s_wait(near(c, s, d)[1], 5, c, s, d)
                s_wait(line(c, s, m), 6, c, s, d)
                s_wait(half_line(c, s, mod4(m - sign[d]), d), 7, c, s, d)

    def stage8(c):
        land(c)
        input_grad(c)

        weight_grad(c)
        settle(c)

    @pl.loop(0, n + 7)
    def _(i):
        for offset, stage in enumerate(
            (stage0, stage1, stage2, stage3, stage4, stage5, stage6, stage7)
        ):
            @pl.when((i >= offset) & (i < n + offset))
            def _(offset=offset, stage=stage):
                stage(i - offset)

            if offset == 0:
                @pl.when(i == 5)
                def _():
                    for cp in sends:
                        cp.wait_send()
                    giacc[...] = jnp.zeros_like(giacc)
                    tok_t[...] = tok[...].reshape(tokens_all, tok.shape[-1]).T

        @pl.when((i >= 8))
        def _():
            stage8(i - 8)

    last = n - 1
    land(last)

    def x_copy(src, dst, which, dev):
        return pltpu.make_async_remote_copy(
            src_ref=src, dst_ref=dst, send_sem=xsem_s.at[which], recv_sem=xsem_r.at[which],
            device_id=dev, device_id_type=MESH,
        )

    cross = []
    for which, zz in enumerate((zo, zp, zm, z)):
        total = None
        for s in (0, 1):
            term = lax.dot_general(
                g[last, s, zz].reshape(4 * slab, part), wv[last, :, cols_of(s)],
                (((1,), (1,)), ((), ())), preferred_element_type=F32,
            )
            total = term if total is None else total + term
        giacc[zz] += total.reshape(2, 2, slab, total.shape[-1])
        cp = x_copy(giacc.at[zz, other], gx.at[zz], which, sib_dev)
        cp.start()
        cross.append(cp)

    wire = zs1.dtype

    def both_cores(zz, h):
        return giacc[zz, core, h] + gx[zz, h]

    cross[0].wait()
    zs1[0, 0] = both_cores(zo, 0).astype(wire)
    zs1[1, 0] = both_cores(zo, 1).astype(wire)
    first = [
        [x_copy(zs1.at[d, ab], zr1.at[d, ab], 4 + 2 * ab + d, z_dev(sign[d])) for d in (0, 1)]
        for ab in (0, 1)
    ]
    first[0][0].start()
    first[0][1].start()
    cross[1].wait()
    zs1[0, 1] = both_cores(zp, 1).astype(wire)
    first[1][0].start()
    cross[2].wait()
    zs1[1, 1] = both_cores(zm, 0).astype(wire)
    first[1][1].start()
    weight_grad(last)
    second = []
    for d in (0, 1):
        first[0][d].wait()
        zsc[d] = (both_cores(mod4(z + sign[d]), d) + zr1[d, 0].astype(F32)).astype(wire)
        cp = x_copy(zsc.at[d], zrc.at[d], 8 + d, z_dev(sign[d]))
        cp.start()
        second.append(cp)
    settle(last)
    cross[3].wait()
    for d in (0, 1):
        first[1][d].wait()
    for d in (0, 1):
        second[d].wait()
        gi_out[pl.ds(d * slab, slab), :] = (
            both_cores(z, d) + zrc[d].astype(F32) + zr1[1 - d, 1].astype(F32)
        ).astype(BF16)


def local(tokens, weight, upstream):
    rows, depth = tokens.shape
    width = weight.shape[1]
    slab = upstream.shape[0]
    n = N_CHUNKS
    part = width // (2 * n)
    half = part // 2
    wire = BF16
    vmem, dma = pltpu.VMEM, pltpu.SemaphoreType.DMA
    scratch = [
        vmem((slab, width), BF16),
        vmem((4, 2, 2, slab, depth), BF16),
        vmem((depth, 16 * slab), BF16),
        vmem((n, depth, 2 * part), BF16),
        vmem((3, 4, 4, slab, 2 * part), F32),
        vmem((n, 2, 2, 2, 2, slab, part), BF16),
        vmem((n, 2, 2, 2, 2, slab, part), BF16),
        vmem((n, 2, 2, 2, slab, part), BF16),
        vmem((n, 2, 2, 2, slab, part), BF16),
        vmem((3, 2, 4, slab, part), F32),
        vmem((n, 2, 2, 2, slab, half), BF16),
        vmem((n, 2, 2, 2, slab, half), BF16),
        vmem((n, 2, 2, slab, half), BF16),
        vmem((n, 2, 2, slab, half), BF16),
        vmem((n, 2, 4, 4, slab, part), BF16),
        vmem((4, 2, 2, slab, depth), F32),
        vmem((4, 2, slab, depth), F32),
        vmem((2, 2, slab, depth), wire),
        vmem((2, 2, slab, depth), wire),
        vmem((2, slab, depth), wire),
        vmem((2, slab, depth), wire),
        dma((n, 2, 8, 2)),
        dma((n, 2, 8, 2)),
        dma((11,)),
        dma((11,)),
        dma((10,)),
        dma((10,)),
        dma((n,)),
        dma((2,)),
    ]
    return pl.pallas_call(
        functools.partial(kernel, n, part, slab),
        out_shape=(
            pltpu.VMEM((rows, depth), BF16),
            pltpu.VMEM((depth, width), BF16),
        ),
        in_specs=[
            pl.BlockSpec(memory_space=pl.ANY),
            pl.BlockSpec(memory_space=pl.ANY),
            pl.BlockSpec(memory_space=pl.ANY),
        ],
        out_specs=(
            pl.BlockSpec(memory_space=pltpu.VMEM),
            pl.BlockSpec(memory_space=pltpu.VMEM),
        ),
        scratch_shapes=scratch,
        compiler_params=pltpu.CompilerParams(
            collective_id=0, has_side_effects=True, vmem_limit_bytes=54 * 1024 * 1024
        ),
        cost_estimate=pl.CostEstimate(
            flops=6 * 16 * slab * depth * width, bytes_accessed=4 * depth * width, transcendentals=slab * width
        ),
    )(tokens.reshape(2, rows // 2, depth), weight, upstream)


def solution(mesh):
    spec = PartitionSpec
    return jax.shard_map(
        local,
        mesh=mesh,
        in_specs=(spec("row", "col"), spec("col", "row"), spec("col", "row")),
        out_specs=(spec("row", "col"), spec("col", "row")),
        check_vma=False,
    )
```

```python
import functools

import jax
import jax.numpy as jnp
from jax import lax
from jax.experimental import pallas as pl
from jax.experimental.pallas import tpu as pltpu
from jax.sharding import PartitionSpec

N_CHUNKS = 5
EARLY = 2
FLUSHES = 8
BF16 = jnp.bfloat16
F32 = jnp.float32
MESH = pl.DeviceIdType.MESH


def gelu_slope(value):
    coeff = 0.7978845608028654
    inner = coeff * (value + 0.044715 * value * value * value)
    tanh_value = jnp.tanh(inner)
    return 0.5 * (1.0 + tanh_value) + 0.5 * value * (1.0 - tanh_value * tanh_value) * coeff * (
        1.0 + 3.0 * 0.044715 * value * value
    )


def mod4(value):
    return lax.rem(value + 4, 4)


def kernel(
    n, part, slab,
    tin, w_hbm, up_hbm, gi_out, gw_out,
    up, tok, tok_t, wv, pf, snd1, rcv1, sndc, rcvc, s2, snd2, rcv2, snd2c, rcv2c, g, giacc,
    gx, zs1, zr1, zsc, zrc,
    ssem, rsem, tsem_s, tsem_r, xsem_s, xsem_r, wsem, lsem,
):
    row, col = lax.axis_index("row"), lax.axis_index("col")
    z, core = lax.div(row, 2), lax.rem(row, 2)
    y, x = lax.div(col, 4), lax.rem(col, 4)
    half = part // 2

    def x_dev(d):
        return {"col": y * 4 + mod4(x + d)}

    def y_dev(d):
        return {"col": mod4(y + d) * 4 + x}

    def z_dev(d):
        return {"row": mod4(z + d) * 2 + core}

    sib_dev = {"row": z * 2 + (1 - core)}
    sign = (1, -1)
    major, minor = (x, y), (y, x)
    major_dev, minor_dev = (x_dev, y_dev), (y_dev, x_dev)

    def at(s, m, k):
        return (k, m) if s == 0 else (m, k)

    def w_copy(c):
        return pltpu.make_async_copy(
            w_hbm.at[:, pl.ds(pl.multiple_of(c * 2 * part, 2 * part), 2 * part)], wv.at[c], wsem.at[c]
        )

    barrier = pltpu.get_barrier_semaphore()
    for dev in (x_dev(1), x_dev(-1), y_dev(1), y_dev(-1), z_dev(1), z_dev(-1), sib_dev):
        pl.semaphore_signal(barrier, inc=1, device_id=dev, device_id_type=MESH)
    own_tok = pltpu.make_async_copy(tin, tok.at[z, core], lsem.at[0])
    own_tok.start()
    for c in range(n):
        w_copy(c).start()
    own_up = pltpu.make_async_copy(up_hbm, up, lsem.at[1])
    own_up.start()
    own_tok.wait()
    pl.semaphore_wait(barrier, 7)

    def t_copy(region, which, dev):
        return pltpu.make_async_remote_copy(
            src_ref=region, dst_ref=region, send_sem=tsem_s.at[which], recv_sem=tsem_r.at[which],
            device_id=dev, device_id_type=MESH,
        )

    def full(zz, cc):
        return tok.at[zz, cc]

    def lo(zz, cc):
        return tok.at[zz, cc, 0]

    def hi(zz, cc):
        return tok.at[zz, cc, 1]

    zm, zp, zo = mod4(z - 1), mod4(z + 1), mod4(z + 2)
    other = 1 - core
    tokens_all = 16 * slab
    sends = []

    def t_send(region, which, dev):
        cp = t_copy(region, which, dev)
        cp.start()
        sends.append(cp)

    def t_wait(region, which):
        t_copy(region, which, sib_dev).wait_recv()

    def r_copy(src, dst, kind, c, s, d, dev):
        return pltpu.make_async_remote_copy(
            src_ref=src, dst_ref=dst, send_sem=ssem.at[c, s, kind, d], recv_sem=rsem.at[c, s, kind, d],
            device_id=dev, device_id_type=MESH,
        )

    def early(zz):
        rows = tok[zz].reshape(4 * slab, tok.shape[-1])
        h, j = lax.div(zz, 2), lax.rem(zz, 2)
        q = mod4(zz - y)
        for c in range(EARLY):
            pf[c, zz] = jnp.dot(rows, wv[c], preferred_element_type=F32).reshape(4, slab, 2 * part)
            for d in (0, 1):
                ab = h if d == 0 else 1 - h
                owner = mod4(x + 2 - h) if d == 0 else mod4(x + 3 - h)
                piece = snd1.at[c, 0, d, ab, j]
                piece[...] = pf[c, zz, owner, :, :part].astype(BF16)
                r_copy(piece, rcv1.at[c, 0, d, ab, j], 0, c, 0, d, x_dev(sign[d])).start()

            def unit(d, ab, k0, c=c):
                snd1[c, 1, d, ab] = pf[c, zz, k0:k0 + 2, :, part:].astype(BF16)
                r_copy(snd1.at[c, 1, d, ab], rcv1.at[c, 1, d, ab], 0, c, 1, d, y_dev(sign[d])).start()

            @pl.when(q == 1)
            def _():
                unit(0, 1, 2)

            @pl.when(q == 2)
            def _():
                unit(0, 0, 0)
                unit(1, 0, 2)

            @pl.when(q == 3)
            def _():
                unit(1, 1, 0)

    t_send(lo(z, core), 0, z_dev(1))
    t_send(hi(z, core), 2, z_dev(-1))
    t_send(hi(z, core), 1, z_dev(1))
    t_send(lo(z, core), 3, z_dev(-1))
    t_send(full(z, core), 4, sib_dev)
    for c in range(EARLY):
        w_copy(c).wait()
    t_wait(full(z, other), 4)
    t_wait(lo(zm, core), 0)
    t_send(lo(zm, core), 5, z_dev(1))
    t_wait(hi(zp, core), 2)
    t_send(hi(zp, core), 6, z_dev(-1))
    early(z)
    t_wait(hi(zm, core), 1)
    t_send(full(zm, core), 7, sib_dev)
    t_wait(lo(zp, core), 3)
    t_send(full(zp, core), 8, sib_dev)
    t_wait(full(zm, other), 7)
    early(zm)
    t_wait(lo(zo, core), 5)
    t_send(lo(zo, core), 9, sib_dev)
    t_wait(hi(zo, core), 6)
    t_send(hi(zo, core), 10, sib_dev)
    t_wait(full(zp, other), 8)
    early(zp)
    t_wait(lo(zo, other), 9)
    t_wait(hi(zo, other), 10)
    early(zo)
    own_up.wait()


    def r_wait(region, kind, c, s, d):
        r_copy(region, region, kind, c, s, d, sib_dev).wait_recv()

    def s_wait(region, kind, c, s, d):
        r_copy(region, region, kind, c, s, d, sib_dev).wait_send()

    def cols_of(s):
        return slice(s * part, (s + 1) * part)

    def stage0(c):
        slot = lax.rem(c, 3)

        w_copy(c).wait()
        out = jnp.dot(
            tok[...].reshape(tokens_all, tok.shape[-1]), wv[c], preferred_element_type=F32
        )
        pf[slot] = out.reshape(4, 4, slab, 2 * part)
        for s in (0, 1):
            m, cols = major[s], cols_of(s)
            for j in (0, 1):
                def piece(mm, k):
                    a, b = at(s, mm, k)
                    return pf[slot, a, b, :, cols].astype(BF16)

                snd1[c, s, 0, 0, j] = piece(mod4(m + 2), j)
                snd1[c, s, 0, 1, j] = piece(mod4(m + 1), 2 + j)
                snd1[c, s, 1, 0, j] = piece(mod4(m + 2), 2 + j)
                snd1[c, s, 1, 1, j] = piece(mod4(m - 1), j)
            for d in (0, 1):
                r_copy(snd1.at[c, s, d], rcv1.at[c, s, d], 0, c, s, d, major_dev[s](sign[d])).start()

    def stage1(c):
        slot = lax.rem(c, 3)
        for s in (0, 1):
            m, cols = major[s], cols_of(s)
            for d in (0, 1):
                r_wait(rcv1.at[c, s, d], 0, c, s, d)
                for j in (0, 1):
                    a, b = at(s, mod4(m + sign[d]), 2 * d + j)
                    sndc[c, s, d, j] = (
                        pf[slot, a, b, :, cols] + rcv1[c, s, d, 0, j].astype(F32)
                    ).astype(BF16)
                r_copy(sndc.at[c, s, d], rcvc.at[c, s, d], 1, c, s, d, major_dev[s](sign[d])).start()

    def stage2(c):
        slot = lax.rem(c, 3)
        for s in (0, 1):
            m, k, cols = major[s], minor[s], cols_of(s)
            for d in (0, 1):
                r_wait(rcvc.at[c, s, d], 1, c, s, d)
            for kk in range(4):
                a, b = at(s, m, kk)
                h, j = kk // 2, kk % 2
                s2[slot, s, kk] = (
                    pf[slot, a, b, :, cols]
                    + rcvc[c, s, h, j].astype(F32)
                    + rcv1[c, s, 1 - h, 1, j].astype(F32)
                )
            lo_c, hi_c = slice(0, half), slice(half, part)
            snd2[c, s, 0, 0] = s2[slot, s, mod4(k + 2), :, lo_c].astype(BF16)
            snd2[c, s, 0, 1] = s2[slot, s, mod4(k + 1), :, hi_c].astype(BF16)
            snd2[c, s, 1, 0] = s2[slot, s, mod4(k + 2), :, hi_c].astype(BF16)
            snd2[c, s, 1, 1] = s2[slot, s, mod4(k - 1), :, lo_c].astype(BF16)
            for d in (0, 1):
                r_copy(snd2.at[c, s, d], rcv2.at[c, s, d], 2, c, s, d, minor_dev[s](sign[d])).start()

    def stage3(c):
        slot = lax.rem(c, 3)
        for s in (0, 1):
            k = minor[s]
            for d in (0, 1):
                r_wait(rcv2.at[c, s, d], 2, c, s, d)
                cols = slice(d * half, (d + 1) * half)
                snd2c[c, s, d] = (
                    s2[slot, s, mod4(k + sign[d]), :, cols] + rcv2[c, s, d, 0].astype(F32)
                ).astype(BF16)
                r_copy(snd2c.at[c, s, d], rcv2c.at[c, s, d], 3, c, s, d, minor_dev[s](sign[d])).start()

    def stage4(c):
        slot = lax.rem(c, 3)
        for s in (0, 1):
            m, k = major[s], minor[s]
            a, b = at(s, m, k)
            for d in (0, 1):
                r_wait(rcv2c.at[c, s, d], 3, c, s, d)
            for h in (0, 1):
                cols = slice(h * half, (h + 1) * half)
                pre = (
                    s2[slot, s, k, :, cols]
                    + rcv2c[c, s, h].astype(F32)
                    + rcv2[c, s, 1 - h, 1].astype(F32)
                )
                at_col = pl.multiple_of(c * 2 * part + s * part + h * half, half)
                upstream = up[:, pl.ds(at_col, half)].astype(F32)
                g[c, s, a, b, :, cols] = (upstream * gelu_slope(pre)).astype(BF16)
            own = g.at[c, s, a, b]
            for d in (0, 1):
                r_copy(own, own, 4, c, s, d, minor_dev[s](sign[d])).start()

    def near(c, s, d):
        a, b = at(s, major[s], mod4(minor[s] - sign[d]))
        return g.at[c, s, a, b], g.at[c, s, a, b, :, pl.ds(d * half, half)]

    def far(c, s, d):
        a, b = at(s, major[s], mod4(minor[s] + 2))
        return g.at[c, s, a, b, :, pl.ds(d * half, half)]

    def stage5(c):
        for s in (0, 1):
            for d in (0, 1):
                whole, onward = near(c, s, d)
                r_wait(whole, 4, c, s, d)
                r_copy(onward, onward, 5, c, s, d, minor_dev[s](sign[d])).start()

    def line(c, s, m):
        return g.at[c, s, :, m] if s == 0 else g.at[c, s, m]

    def half_line(c, s, m, d):
        return g.at[c, s, pl.ds(2 * d, 2), m] if s == 0 else g.at[c, s, m, pl.ds(2 * d, 2)]

    def stage6(c):
        for s in (0, 1):
            for d in (0, 1):
                r_wait(far(c, s, d), 5, c, s, d)
            own = line(c, s, major[s])
            for d in (0, 1):
                r_copy(own, own, 6, c, s, d, major_dev[s](sign[d])).start()

    def stage7(c):
        for s in (0, 1):
            for d in (0, 1):
                m = mod4(major[s] - sign[d])
                r_wait(line(c, s, m), 6, c, s, d)
                onward = half_line(c, s, m, d)
                r_copy(onward, onward, 7, c, s, d, major_dev[s](sign[d])).start()

    def grad_of(c, s):
        return g[c, s].reshape(tokens_all, part)

    def land(c):
        for s in (0, 1):
            for d in (0, 1):
                r_wait(half_line(c, s, mod4(major[s] + 2), d), 7, c, s, d)

    def input_grad(c):
        total = None
        for s in (0, 1):
            term = lax.dot_general(
                grad_of(c, s), wv[c, :, cols_of(s)], (((1,), (1,)), ((), ())), preferred_element_type=F32
            )
            total = term if total is None else total + term
        giacc[...] += total.reshape(giacc.shape)

    def weight_grad(c):
        for s in (0, 1):
            gw_out[:, pl.ds(pl.multiple_of((c * 2 + s) * part, part), part)] = jnp.dot(
                tok_t[...], grad_of(c, s), preferred_element_type=F32
            ).astype(BF16)

    def settle(c):
        for s in (0, 1):
            m, k = major[s], minor[s]
            a, b = at(s, m, k)
            for d in (0, 1):
                s_wait(snd1.at[c, s, d], 0, c, s, d)
                s_wait(sndc.at[c, s, d], 1, c, s, d)
                s_wait(snd2.at[c, s, d], 2, c, s, d)
                s_wait(snd2c.at[c, s, d], 3, c, s, d)
                s_wait(g.at[c, s, a, b], 4, c, s, d)
                s_wait(near(c, s, d)[1], 5, c, s, d)
                s_wait(line(c, s, m), 6, c, s, d)
                s_wait(half_line(c, s, mod4(m - sign[d]), d), 7, c, s, d)

    def stage8(c):
        land(c)
        input_grad(c)

        weight_grad(c)
        settle(c)

    @pl.loop(1, n + 7)
    def _(i):
        for offset, stage in enumerate(
            (stage0, stage1, stage2, stage3, stage4, stage5, stage6, stage7)
        ):
            start = EARLY if offset == 0 else 0

            @pl.when((i >= offset + start) & (i < n + offset))
            def _(offset=offset, stage=stage):
                stage(i - offset)

            if offset == 0:
                @pl.when(i == 5)
                def _():
                    for cp in sends:
                        cp.wait_send()
                    giacc[...] = jnp.zeros_like(giacc)
                    tok_t[...] = tok[...].reshape(tokens_all, tok.shape[-1]).T

        @pl.when((i >= 8))
        def _():
            stage8(i - 8)

    last = n - 1
    land(last)

    def x_copy(src, dst, which, dev):
        return pltpu.make_async_remote_copy(
            src_ref=src, dst_ref=dst, send_sem=xsem_s.at[which], recv_sem=xsem_r.at[which],
            device_id=dev, device_id_type=MESH,
        )

    cross = []
    for which, zz in enumerate((zo, zp, zm, z)):
        total = None
        for s in (0, 1):
            term = lax.dot_general(
                g[last, s, zz].reshape(4 * slab, part), wv[last, :, cols_of(s)],
                (((1,), (1,)), ((), ())), preferred_element_type=F32,
            )
            total = term if total is None else total + term
        giacc[zz] += total.reshape(2, 2, slab, total.shape[-1])
        cp = x_copy(giacc.at[zz, other], gx.at[zz], which, sib_dev)
        cp.start()
        cross.append(cp)

    wire = zs1.dtype

    def both_cores(zz, h):
        return giacc[zz, core, h] + gx[zz, h]

    cross[0].wait()
    zs1[0, 0] = both_cores(zo, 0).astype(wire)
    zs1[1, 0] = both_cores(zo, 1).astype(wire)
    first = [
        [x_copy(zs1.at[d, ab], zr1.at[d, ab], 4 + 2 * ab + d, z_dev(sign[d])) for d in (0, 1)]
        for ab in (0, 1)
    ]
    first[0][0].start()
    first[0][1].start()
    cross[1].wait()
    zs1[0, 1] = both_cores(zp, 1).astype(wire)
    first[1][0].start()
    cross[2].wait()
    zs1[1, 1] = both_cores(zm, 0).astype(wire)
    first[1][1].start()
    weight_grad(last)
    second = []
    for d in (0, 1):
        first[0][d].wait()
        zsc[d] = (both_cores(mod4(z + sign[d]), d) + zr1[d, 0].astype(F32)).astype(wire)
        cp = x_copy(zsc.at[d], zrc.at[d], 8 + d, z_dev(sign[d]))
        cp.start()
        second.append(cp)
    settle(last)
    cross[3].wait()
    for d in (0, 1):
        first[1][d].wait()
    for d in (0, 1):
        second[d].wait()
        gi_out[pl.ds(d * slab, slab), :] = (
            both_cores(z, d) + zrc[d].astype(F32) + zr1[1 - d, 1].astype(F32)
        ).astype(BF16)


def flush(gi, gw, gi_out, gw_out, sem):
    step = gw.shape[0] // FLUSHES
    copies = [pltpu.make_async_copy(gi, gi_out, sem.at[FLUSHES])]
    for j in range(FLUSHES):
        rows = pl.ds(j * step, step)
        copies.append(pltpu.make_async_copy(gw.at[rows], gw_out.at[rows], sem.at[j]))
    for cp in copies:
        cp.start()
    for cp in copies:
        cp.wait()


def local(tokens, weight, upstream):
    rows, depth = tokens.shape
    width = weight.shape[1]
    slab = upstream.shape[0]
    n = N_CHUNKS
    part = width // (2 * n)
    half = part // 2
    wire = BF16
    vmem, dma = pltpu.VMEM, pltpu.SemaphoreType.DMA
    scratch = [
        vmem((slab, width), BF16),
        vmem((4, 2, 2, slab, depth), BF16),
        vmem((depth, 16 * slab), BF16),
        vmem((n, depth, 2 * part), BF16),
        vmem((3, 4, 4, slab, 2 * part), F32),
        vmem((n, 2, 2, 2, 2, slab, part), BF16),
        vmem((n, 2, 2, 2, 2, slab, part), BF16),
        vmem((n, 2, 2, 2, slab, part), BF16),
        vmem((n, 2, 2, 2, slab, part), BF16),
        vmem((3, 2, 4, slab, part), F32),
        vmem((n, 2, 2, 2, slab, half), BF16),
        vmem((n, 2, 2, 2, slab, half), BF16),
        vmem((n, 2, 2, slab, half), BF16),
        vmem((n, 2, 2, slab, half), BF16),
        vmem((n, 2, 4, 4, slab, part), BF16),
        vmem((4, 2, 2, slab, depth), F32),
        vmem((4, 2, slab, depth), F32),
        vmem((2, 2, slab, depth), wire),
        vmem((2, 2, slab, depth), wire),
        vmem((2, slab, depth), wire),
        vmem((2, slab, depth), wire),
        dma((n, 2, 8, 2)),
        dma((n, 2, 8, 2)),
        dma((11,)),
        dma((11,)),
        dma((10,)),
        dma((10,)),
        dma((n,)),
        dma((2,)),
    ]
    gi, gw = pl.pallas_call(
        functools.partial(kernel, n, part, slab),
        out_shape=(
            pltpu.VMEM((rows, depth), BF16),
            pltpu.VMEM((depth, width), BF16),
        ),
        in_specs=[
            pl.BlockSpec(memory_space=pl.ANY),
            pl.BlockSpec(memory_space=pl.ANY),
            pl.BlockSpec(memory_space=pl.ANY),
        ],
        out_specs=(
            pl.BlockSpec(memory_space=pltpu.VMEM),
            pl.BlockSpec(memory_space=pltpu.VMEM),
        ),
        scratch_shapes=scratch,
        compiler_params=pltpu.CompilerParams(
            collective_id=0, has_side_effects=True, vmem_limit_bytes=54 * 1024 * 1024
        ),
        cost_estimate=pl.CostEstimate(
            flops=6 * 16 * slab * depth * width, bytes_accessed=4 * depth * width, transcendentals=slab * width
        ),
    )(tokens.reshape(2, rows // 2, depth), weight, upstream)

    return pl.pallas_call(
        flush,
        out_shape=(
            jax.ShapeDtypeStruct((rows, depth), BF16),
            jax.ShapeDtypeStruct((depth, width), BF16),
        ),
        in_specs=[pl.BlockSpec(memory_space=pltpu.VMEM)] * 2,
        out_specs=(pl.BlockSpec(memory_space=pl.ANY),) * 2,
        scratch_shapes=[dma((FLUSHES + 1,))],
        compiler_params=pltpu.CompilerParams(vmem_limit_bytes=1024 * 1024),
    )(pltpu.with_memory_space_constraint(gi, pltpu.VMEM), pltpu.with_memory_space_constraint(gw, pltpu.VMEM))


def solution(mesh):
    spec = PartitionSpec
    return jax.shard_map(
        local,
        mesh=mesh,
        in_specs=(spec("row", "col"), spec("col", "row"), spec("col", "row")),
        out_specs=(spec("row", "col"), spec("col", "row")),
        check_vma=False,
    )
```

```python
import functools

import jax
import jax.numpy as jnp
from jax import lax
from jax.experimental import pallas as pl
from jax.experimental.pallas import tpu as pltpu
from jax.sharding import PartitionSpec

N_CHUNKS = 5
EARLY = 2
FLUSHES = 8
BF16 = jnp.bfloat16
F32 = jnp.float32
MESH = pl.DeviceIdType.MESH


def gelu_slope(value):
    coeff = 0.7978845608028654
    inner = coeff * (value + 0.044715 * value * value * value)
    tanh_value = jnp.tanh(inner)
    return 0.5 * (1.0 + tanh_value) + 0.5 * value * (1.0 - tanh_value * tanh_value) * coeff * (
        1.0 + 3.0 * 0.044715 * value * value
    )


def mod4(value):
    return lax.rem(value + 4, 4)


def kernel(
    n, part, slab,
    tin, w_hbm, up_hbm, gi_out, gw_out,
    up, tok, tok_t, wv, pf, snd1, rcv1, sndc, rcvc, s2, snd2, rcv2, snd2c, rcv2c, g, giacc,
    gx, zs1, zr1, zsc, zrc,
    ssem, rsem, tsem_s, tsem_r, xsem_s, xsem_r, wsem, lsem,
):
    row, col = lax.axis_index("row"), lax.axis_index("col")
    z, core = lax.div(row, 2), lax.rem(row, 2)
    y, x = lax.div(col, 4), lax.rem(col, 4)
    half = part // 2

    def x_dev(d):
        return {"col": y * 4 + mod4(x + d)}

    def y_dev(d):
        return {"col": mod4(y + d) * 4 + x}

    def z_dev(d):
        return {"row": mod4(z + d) * 2 + core}

    sib_dev = {"row": z * 2 + (1 - core)}
    sign = (1, -1)
    major, minor = (x, y), (y, x)
    major_dev, minor_dev = (x_dev, y_dev), (y_dev, x_dev)

    def at(s, m, k):
        return (k, m) if s == 0 else (m, k)

    def w_copy(c):
        return pltpu.make_async_copy(
            w_hbm.at[:, pl.ds(pl.multiple_of(c * 2 * part, 2 * part), 2 * part)], wv.at[c], wsem.at[c]
        )

    barrier = pltpu.get_barrier_semaphore()
    for dev in (x_dev(1), x_dev(-1), y_dev(1), y_dev(-1), z_dev(1), z_dev(-1), sib_dev):
        pl.semaphore_signal(barrier, inc=1, device_id=dev, device_id_type=MESH)
    own_tok = pltpu.make_async_copy(tin, tok.at[z, core], lsem.at[0])
    own_tok.start()
    for c in range(n):
        w_copy(c).start()
    own_up = pltpu.make_async_copy(up_hbm, up, lsem.at[1])
    own_up.start()
    own_tok.wait()
    pl.semaphore_wait(barrier, 7)

    def t_copy(region, which, dev):
        return pltpu.make_async_remote_copy(
            src_ref=region, dst_ref=region, send_sem=tsem_s.at[which], recv_sem=tsem_r.at[which],
            device_id=dev, device_id_type=MESH,
        )

    def full(zz, cc):
        return tok.at[zz, cc]

    def lo(zz, cc):
        return tok.at[zz, cc, 0]

    def hi(zz, cc):
        return tok.at[zz, cc, 1]

    zm, zp, zo = mod4(z - 1), mod4(z + 1), mod4(z + 2)
    other = 1 - core
    tokens_all = 16 * slab
    sends = []

    def t_send(region, which, dev):
        cp = t_copy(region, which, dev)
        cp.start()
        sends.append(cp)

    def t_wait(region, which):
        t_copy(region, which, sib_dev).wait_recv()

    def r_copy(src, dst, kind, c, s, d, dev):
        return pltpu.make_async_remote_copy(
            src_ref=src, dst_ref=dst, send_sem=ssem.at[c, s, kind, d], recv_sem=rsem.at[c, s, kind, d],
            device_id=dev, device_id_type=MESH,
        )

    def early(zz):
        rows = tok[zz].reshape(4 * slab, tok.shape[-1])
        h, j = lax.div(zz, 2), lax.rem(zz, 2)
        q = mod4(zz - y)
        for c in range(EARLY):
            pf[c, zz] = jnp.dot(rows, wv[c], preferred_element_type=F32).reshape(4, slab, 2 * part)
            for d in (0, 1):
                ab = h if d == 0 else 1 - h
                owner = mod4(x + 2 - h) if d == 0 else mod4(x + 3 - h)
                piece = snd1.at[c, 0, d, ab, j]
                piece[...] = pf[c, zz, owner, :, :part].astype(BF16)
                r_copy(piece, rcv1.at[c, 0, d, ab, j], 0, c, 0, d, x_dev(sign[d])).start()

            def unit(d, ab, k0, c=c):
                snd1[c, 1, d, ab] = pf[c, zz, k0:k0 + 2, :, part:].astype(BF16)
                r_copy(snd1.at[c, 1, d, ab], rcv1.at[c, 1, d, ab], 0, c, 1, d, y_dev(sign[d])).start()

            @pl.when(q == 1)
            def _():
                unit(0, 1, 2)

            @pl.when(q == 2)
            def _():
                unit(0, 0, 0)
                unit(1, 0, 2)

            @pl.when(q == 3)
            def _():
                unit(1, 1, 0)

    t_send(lo(z, core), 0, z_dev(1))
    t_send(hi(z, core), 2, z_dev(-1))
    t_send(hi(z, core), 1, z_dev(1))
    t_send(lo(z, core), 3, z_dev(-1))
    t_send(full(z, core), 4, sib_dev)
    for c in range(EARLY):
        w_copy(c).wait()
    t_wait(full(z, other), 4)
    t_wait(lo(zm, core), 0)
    t_send(lo(zm, core), 5, z_dev(1))
    t_wait(hi(zp, core), 2)
    t_send(hi(zp, core), 6, z_dev(-1))
    early(z)
    t_wait(hi(zm, core), 1)
    t_send(full(zm, core), 7, sib_dev)
    t_wait(lo(zp, core), 3)
    t_send(full(zp, core), 8, sib_dev)
    t_wait(full(zm, other), 7)
    early(zm)
    t_wait(lo(zo, core), 5)
    t_send(lo(zo, core), 9, sib_dev)
    t_wait(hi(zo, core), 6)
    t_send(hi(zo, core), 10, sib_dev)
    t_wait(full(zp, other), 8)
    early(zp)
    t_wait(lo(zo, other), 9)
    t_wait(hi(zo, other), 10)
    early(zo)
    own_up.wait()


    def r_wait(region, kind, c, s, d):
        r_copy(region, region, kind, c, s, d, sib_dev).wait_recv()

    def s_wait(region, kind, c, s, d):
        r_copy(region, region, kind, c, s, d, sib_dev).wait_send()

    def cols_of(s):
        return slice(s * part, (s + 1) * part)

    def stage0(c):
        slot = lax.rem(c, 3)

        w_copy(c).wait()
        out = jnp.dot(
            tok[...].reshape(tokens_all, tok.shape[-1]), wv[c], preferred_element_type=F32
        )
        pf[lax.rem(c, 4)] = out.reshape(4, 4, slab, 2 * part)
        for s in (0, 1):
            m, cols = major[s], cols_of(s)
            for j in (0, 1):
                def piece(mm, k):
                    a, b = at(s, mm, k)
                    return pf[lax.rem(c, 4), a, b, :, cols].astype(BF16)

                snd1[c, s, 0, 0, j] = piece(mod4(m + 2), j)
                snd1[c, s, 0, 1, j] = piece(mod4(m + 1), 2 + j)
                snd1[c, s, 1, 0, j] = piece(mod4(m + 2), 2 + j)
                snd1[c, s, 1, 1, j] = piece(mod4(m - 1), j)
            for d in (0, 1):
                r_copy(snd1.at[c, s, d], rcv1.at[c, s, d], 0, c, s, d, major_dev[s](sign[d])).start()

    def stage1(c):
        slot = lax.rem(c, 3)
        for s in (0, 1):
            m, cols = major[s], cols_of(s)
            for d in (0, 1):
                r_wait(rcv1.at[c, s, d], 0, c, s, d)
                for j in (0, 1):
                    a, b = at(s, mod4(m + sign[d]), 2 * d + j)
                    sndc[c, s, d, j] = (
                        pf[lax.rem(c, 4), a, b, :, cols] + rcv1[c, s, d, 0, j].astype(F32)
                    ).astype(BF16)
                r_copy(sndc.at[c, s, d], rcvc.at[c, s, d], 1, c, s, d, major_dev[s](sign[d])).start()

    def stage2(c):
        slot = lax.rem(c, 3)
        for s in (0, 1):
            m, k, cols = major[s], minor[s], cols_of(s)
            for d in (0, 1):
                r_wait(rcvc.at[c, s, d], 1, c, s, d)
            for kk in range(4):
                a, b = at(s, m, kk)
                h, j = kk // 2, kk % 2
                s2[slot, s, kk] = (
                    pf[lax.rem(c, 4), a, b, :, cols]
                    + rcvc[c, s, h, j].astype(F32)
                    + rcv1[c, s, 1 - h, 1, j].astype(F32)
                )
            lo_c, hi_c = slice(0, half), slice(half, part)
            snd2[c, s, 0, 0] = s2[slot, s, mod4(k + 2), :, lo_c].astype(BF16)
            snd2[c, s, 0, 1] = s2[slot, s, mod4(k + 1), :, hi_c].astype(BF16)
            snd2[c, s, 1, 0] = s2[slot, s, mod4(k + 2), :, hi_c].astype(BF16)
            snd2[c, s, 1, 1] = s2[slot, s, mod4(k - 1), :, lo_c].astype(BF16)
            for d in (0, 1):
                r_copy(snd2.at[c, s, d], rcv2.at[c, s, d], 2, c, s, d, minor_dev[s](sign[d])).start()

    def stage3(c):
        slot = lax.rem(c, 3)
        for s in (0, 1):
            k = minor[s]
            for d in (0, 1):
                r_wait(rcv2.at[c, s, d], 2, c, s, d)
                cols = slice(d * half, (d + 1) * half)
                snd2c[c, s, d] = (
                    s2[slot, s, mod4(k + sign[d]), :, cols] + rcv2[c, s, d, 0].astype(F32)
                ).astype(BF16)
                r_copy(snd2c.at[c, s, d], rcv2c.at[c, s, d], 3, c, s, d, minor_dev[s](sign[d])).start()

    def stage4(c):
        slot = lax.rem(c, 3)
        for s in (0, 1):
            m, k = major[s], minor[s]
            a, b = at(s, m, k)
            for d in (0, 1):
                r_wait(rcv2c.at[c, s, d], 3, c, s, d)
            for h in (0, 1):
                cols = slice(h * half, (h + 1) * half)
                pre = (
                    s2[slot, s, k, :, cols]
                    + rcv2c[c, s, h].astype(F32)
                    + rcv2[c, s, 1 - h, 1].astype(F32)
                )
                at_col = pl.multiple_of(c * 2 * part + s * part + h * half, half)
                upstream = up[:, pl.ds(at_col, half)].astype(F32)
                g[c, s, a, b, :, cols] = (upstream * gelu_slope(pre)).astype(BF16)
            own = g.at[c, s, a, b]
            for d in (0, 1):
                r_copy(own, own, 4, c, s, d, minor_dev[s](sign[d])).start()

    def near(c, s, d):
        a, b = at(s, major[s], mod4(minor[s] - sign[d]))
        return g.at[c, s, a, b], g.at[c, s, a, b, :, pl.ds(d * half, half)]

    def far(c, s, d):
        a, b = at(s, major[s], mod4(minor[s] + 2))
        return g.at[c, s, a, b, :, pl.ds(d * half, half)]

    def stage5(c):
        for s in (0, 1):
            for d in (0, 1):
                whole, onward = near(c, s, d)
                r_wait(whole, 4, c, s, d)
                r_copy(onward, onward, 5, c, s, d, minor_dev[s](sign[d])).start()

    def line(c, s, m):
        return g.at[c, s, :, m] if s == 0 else g.at[c, s, m]

    def half_line(c, s, m, d):
        return g.at[c, s, pl.ds(2 * d, 2), m] if s == 0 else g.at[c, s, m, pl.ds(2 * d, 2)]

    def stage6(c):
        for s in (0, 1):
            for d in (0, 1):
                r_wait(far(c, s, d), 5, c, s, d)
            own = line(c, s, major[s])
            for d in (0, 1):
                r_copy(own, own, 6, c, s, d, major_dev[s](sign[d])).start()

    def stage7(c):
        for s in (0, 1):
            for d in (0, 1):
                m = mod4(major[s] - sign[d])
                r_wait(line(c, s, m), 6, c, s, d)
                onward = half_line(c, s, m, d)
                r_copy(onward, onward, 7, c, s, d, major_dev[s](sign[d])).start()

    def grad_of(c, s):
        return g[c, s].reshape(tokens_all, part)

    def land(c):
        for s in (0, 1):
            for d in (0, 1):
                r_wait(half_line(c, s, mod4(major[s] + 2), d), 7, c, s, d)

    def input_grad(c):
        total = None
        for s in (0, 1):
            term = lax.dot_general(
                grad_of(c, s), wv[c, :, cols_of(s)], (((1,), (1,)), ((), ())), preferred_element_type=F32
            )
            total = term if total is None else total + term
        giacc[...] += total.reshape(giacc.shape)

    def weight_grad(c):
        for s in (0, 1):
            gw_out[:, pl.ds(pl.multiple_of((c * 2 + s) * part, part), part)] = jnp.dot(
                tok_t[...], grad_of(c, s), preferred_element_type=F32
            ).astype(BF16)

    def settle(c):
        for s in (0, 1):
            m, k = major[s], minor[s]
            a, b = at(s, m, k)
            for d in (0, 1):
                s_wait(snd1.at[c, s, d], 0, c, s, d)
                s_wait(sndc.at[c, s, d], 1, c, s, d)
                s_wait(snd2.at[c, s, d], 2, c, s, d)
                s_wait(snd2c.at[c, s, d], 3, c, s, d)
                s_wait(g.at[c, s, a, b], 4, c, s, d)
                s_wait(near(c, s, d)[1], 5, c, s, d)
                s_wait(line(c, s, m), 6, c, s, d)
                s_wait(half_line(c, s, mod4(m - sign[d]), d), 7, c, s, d)

    def stage8(c):
        land(c)
        input_grad(c)

        weight_grad(c)
        settle(c)

    @pl.loop(1, n + 6)
    def _(i):
        for offset, stage in enumerate(
            (stage0, stage1, stage2, stage3, stage4, stage5, stage6, stage7)
        ):
            shift = offset if offset else -1
            start = EARLY if offset == 0 else 0

            @pl.when((i >= shift + start) & (i < n + shift))
            def _(shift=shift, stage=stage):
                stage(i - shift)

            if offset == 0:
                @pl.when(i == 5)
                def _():
                    for cp in sends:
                        cp.wait_send()
                    giacc[...] = jnp.zeros_like(giacc)
                    tok_t[...] = tok[...].reshape(tokens_all, tok.shape[-1]).T

        @pl.when((i >= 8))
        def _():
            stage8(i - 8)

    last = n - 1
    stage7(last)
    land(last - 1)
    input_grad(last - 1)
    land(last)

    def x_copy(src, dst, which, dev):
        return pltpu.make_async_remote_copy(
            src_ref=src, dst_ref=dst, send_sem=xsem_s.at[which], recv_sem=xsem_r.at[which],
            device_id=dev, device_id_type=MESH,
        )

    cross = []
    for which, zz in enumerate((zo, zp, zm, z)):
        total = None
        for s in (0, 1):
            term = lax.dot_general(
                g[last, s, zz].reshape(4 * slab, part), wv[last, :, cols_of(s)],
                (((1,), (1,)), ((), ())), preferred_element_type=F32,
            )
            total = term if total is None else total + term
        giacc[zz] += total.reshape(2, 2, slab, total.shape[-1])
        cp = x_copy(giacc.at[zz, other], gx.at[zz], which, sib_dev)
        cp.start()
        cross.append(cp)

    wire = zs1.dtype

    def both_cores(zz, h):
        return giacc[zz, core, h] + gx[zz, h]

    cross[0].wait()
    zs1[0, 0] = both_cores(zo, 0).astype(wire)
    zs1[1, 0] = both_cores(zo, 1).astype(wire)
    first = [
        [x_copy(zs1.at[d, ab], zr1.at[d, ab], 4 + 2 * ab + d, z_dev(sign[d])) for d in (0, 1)]
        for ab in (0, 1)
    ]
    first[0][0].start()
    first[0][1].start()
    cross[1].wait()
    zs1[0, 1] = both_cores(zp, 1).astype(wire)
    first[1][0].start()
    cross[2].wait()
    zs1[1, 1] = both_cores(zm, 0).astype(wire)
    first[1][1].start()
    weight_grad(last - 1)
    second = []
    for d in (0, 1):
        first[0][d].wait()
        zsc[d] = (both_cores(mod4(z + sign[d]), d) + zr1[d, 0].astype(F32)).astype(wire)
        cp = x_copy(zsc.at[d], zrc.at[d], 8 + d, z_dev(sign[d]))
        cp.start()
        second.append(cp)
    weight_grad(last)
    settle(last - 1)
    settle(last)
    cross[3].wait()
    for d in (0, 1):
        first[1][d].wait()
    for d in (0, 1):
        second[d].wait()
        gi_out[pl.ds(d * slab, slab), :] = (
            both_cores(z, d) + zrc[d].astype(F32) + zr1[1 - d, 1].astype(F32)
        ).astype(BF16)


def flush(gi, gw, gi_out, gw_out, sem):
    step = gw.shape[0] // FLUSHES
    copies = [pltpu.make_async_copy(gi, gi_out, sem.at[FLUSHES])]
    for j in range(FLUSHES):
        rows = pl.ds(j * step, step)
        copies.append(pltpu.make_async_copy(gw.at[rows], gw_out.at[rows], sem.at[j]))
    for cp in copies:
        cp.start()
    for cp in copies:
        cp.wait()


def local(tokens, weight, upstream):
    rows, depth = tokens.shape
    width = weight.shape[1]
    slab = upstream.shape[0]
    n = N_CHUNKS
    part = width // (2 * n)
    half = part // 2
    wire = BF16
    vmem, dma = pltpu.VMEM, pltpu.SemaphoreType.DMA
    scratch = [
        vmem((slab, width), BF16),
        vmem((4, 2, 2, slab, depth), BF16),
        vmem((depth, 16 * slab), BF16),
        vmem((n, depth, 2 * part), BF16),
        vmem((4, 4, 4, slab, 2 * part), F32),
        vmem((n, 2, 2, 2, 2, slab, part), BF16),
        vmem((n, 2, 2, 2, 2, slab, part), BF16),
        vmem((n, 2, 2, 2, slab, part), BF16),
        vmem((n, 2, 2, 2, slab, part), BF16),
        vmem((3, 2, 4, slab, part), F32),
        vmem((n, 2, 2, 2, slab, half), BF16),
        vmem((n, 2, 2, 2, slab, half), BF16),
        vmem((n, 2, 2, slab, half), BF16),
        vmem((n, 2, 2, slab, half), BF16),
        vmem((n, 2, 4, 4, slab, part), BF16),
        vmem((4, 2, 2, slab, depth), F32),
        vmem((4, 2, slab, depth), F32),
        vmem((2, 2, slab, depth), wire),
        vmem((2, 2, slab, depth), wire),
        vmem((2, slab, depth), wire),
        vmem((2, slab, depth), wire),
        dma((n, 2, 8, 2)),
        dma((n, 2, 8, 2)),
        dma((11,)),
        dma((11,)),
        dma((10,)),
        dma((10,)),
        dma((n,)),
        dma((2,)),
    ]
    gi, gw = pl.pallas_call(
        functools.partial(kernel, n, part, slab),
        out_shape=(
            pltpu.VMEM((rows, depth), BF16),
            pltpu.VMEM((depth, width), BF16),
        ),
        in_specs=[
            pl.BlockSpec(memory_space=pl.ANY),
            pl.BlockSpec(memory_space=pl.ANY),
            pl.BlockSpec(memory_space=pl.ANY),
        ],
        out_specs=(
            pl.BlockSpec(memory_space=pltpu.VMEM),
            pl.BlockSpec(memory_space=pltpu.VMEM),
        ),
        scratch_shapes=scratch,
        compiler_params=pltpu.CompilerParams(
            collective_id=0, has_side_effects=True, vmem_limit_bytes=56 * 1024 * 1024 + 512 * 1024
        ),
        cost_estimate=pl.CostEstimate(
            flops=6 * 16 * slab * depth * width, bytes_accessed=4 * depth * width, transcendentals=slab * width
        ),
    )(tokens.reshape(2, rows // 2, depth), weight, upstream)

    return pl.pallas_call(
        flush,
        out_shape=(
            jax.ShapeDtypeStruct((rows, depth), BF16),
            jax.ShapeDtypeStruct((depth, width), BF16),
        ),
        in_specs=[pl.BlockSpec(memory_space=pltpu.VMEM)] * 2,
        out_specs=(pl.BlockSpec(memory_space=pl.ANY),) * 2,
        scratch_shapes=[dma((FLUSHES + 1,))],
        compiler_params=pltpu.CompilerParams(vmem_limit_bytes=1024 * 1024),
    )(pltpu.with_memory_space_constraint(gi, pltpu.VMEM), pltpu.with_memory_space_constraint(gw, pltpu.VMEM))


def solution(mesh):
    spec = PartitionSpec
    return jax.shard_map(
        local,
        mesh=mesh,
        in_specs=(spec("row", "col"), spec("col", "row"), spec("col", "row")),
        out_specs=(spec("row", "col"), spec("col", "row")),
        check_vma=False,
    )
```

```python
import functools

import jax
import jax.numpy as jnp
from jax import lax
from jax.experimental import pallas as pl
from jax.experimental.pallas import tpu as pltpu
from jax.sharding import PartitionSpec

N_CHUNKS = 5
EARLY = 2
FLUSHES = 8
BF16 = jnp.bfloat16
F32 = jnp.float32
MESH = pl.DeviceIdType.MESH


def gelu_slope(value):
    coeff = 0.7978845608028654
    inner = coeff * (value + 0.044715 * value * value * value)
    tanh_value = jnp.tanh(inner)
    return 0.5 * (1.0 + tanh_value) + 0.5 * value * (1.0 - tanh_value * tanh_value) * coeff * (
        1.0 + 3.0 * 0.044715 * value * value
    )


def mod4(value):
    return lax.rem(value + 4, 4)


def kernel(
    n, part, slab,
    tin, w_hbm, up_hbm, gi_out, gw_out,
    up, tok, tok_t, wv, pf, snd1, rcv1, sndc, rcvc, s2, snd2, rcv2, snd2c, rcv2c, g, giacc,
    gx, zs1, zr1, zsc, zrc,
    ssem, rsem, tsem_s, tsem_r, xsem_s, xsem_r, wsem, lsem,
):
    row, col = lax.axis_index("row"), lax.axis_index("col")
    z, core = lax.div(row, 2), lax.rem(row, 2)
    y, x = lax.div(col, 4), lax.rem(col, 4)
    half = part // 2

    def x_dev(d):
        return {"col": y * 4 + mod4(x + d)}

    def y_dev(d):
        return {"col": mod4(y + d) * 4 + x}

    def z_dev(d):
        return {"row": mod4(z + d) * 2 + core}

    sib_dev = {"row": z * 2 + (1 - core)}
    sign = (1, -1)
    major, minor = (x, y), (y, x)
    major_dev, minor_dev = (x_dev, y_dev), (y_dev, x_dev)

    def at(s, m, k):
        return (k, m) if s == 0 else (m, k)

    def w_copy(c):
        return pltpu.make_async_copy(
            w_hbm.at[:, pl.ds(pl.multiple_of(c * 2 * part, 2 * part), 2 * part)], wv.at[c], wsem.at[c]
        )

    barrier = pltpu.get_barrier_semaphore()
    for dev in (x_dev(1), x_dev(-1), y_dev(1), y_dev(-1), z_dev(1), z_dev(-1), sib_dev):
        pl.semaphore_signal(barrier, inc=1, device_id=dev, device_id_type=MESH)
    own_tok = pltpu.make_async_copy(tin, tok.at[z, core], lsem.at[0])
    own_tok.start()
    for c in range(n):
        w_copy(c).start()
    own_up = pltpu.make_async_copy(up_hbm, up, lsem.at[1])
    own_up.start()
    pl.semaphore_wait(barrier, 7)

    def t_copy(region, which, dev, src=None):
        return pltpu.make_async_remote_copy(
            src_ref=region if src is None else src, dst_ref=region, send_sem=tsem_s.at[which], recv_sem=tsem_r.at[which],
            device_id=dev, device_id_type=MESH,
        )

    def full(zz, cc):
        return tok.at[zz, cc]

    def lo(zz, cc):
        return tok.at[zz, cc, 0]

    def hi(zz, cc):
        return tok.at[zz, cc, 1]

    zm, zp, zo = mod4(z - 1), mod4(z + 1), mod4(z + 2)
    other = 1 - core
    tokens_all = 16 * slab
    sends = []

    def t_send(region, which, dev, src=None):
        cp = t_copy(region, which, dev, src)
        cp.start()
        sends.append(cp)

    def t_wait(region, which):
        t_copy(region, which, sib_dev).wait_recv()

    def r_copy(src, dst, kind, c, s, d, dev):
        return pltpu.make_async_remote_copy(
            src_ref=src, dst_ref=dst, send_sem=ssem.at[c, s, kind, d], recv_sem=rsem.at[c, s, kind, d],
            device_id=dev, device_id_type=MESH,
        )

    def early(zz):
        rows = tok[zz].reshape(4 * slab, tok.shape[-1])
        h, j = lax.div(zz, 2), lax.rem(zz, 2)
        q = mod4(zz - y)
        for c in range(EARLY):
            pf[c, zz] = jnp.dot(rows, wv[c], preferred_element_type=F32).reshape(4, slab, 2 * part)
            for d in (0, 1):
                ab = h if d == 0 else 1 - h
                owner = mod4(x + 2 - h) if d == 0 else mod4(x + 3 - h)
                piece = snd1.at[c, 0, d, ab, j]
                piece[...] = pf[c, zz, owner, :, :part].astype(BF16)
                r_copy(piece, rcv1.at[c, 0, d, ab, j], 0, c, 0, d, x_dev(sign[d])).start()

            def unit(d, ab, k0, c=c):
                snd1[c, 1, d, ab] = pf[c, zz, k0:k0 + 2, :, part:].astype(BF16)
                r_copy(snd1.at[c, 1, d, ab], rcv1.at[c, 1, d, ab], 0, c, 1, d, y_dev(sign[d])).start()

            @pl.when(q == 1)
            def _():
                unit(0, 1, 2)

            @pl.when(q == 2)
            def _():
                unit(0, 0, 0)
                unit(1, 0, 2)

            @pl.when(q == 3)
            def _():
                unit(1, 1, 0)

    for src, dst, which, dev in (
        (tin.at[0], lo(z, core), 0, z_dev(1)),
        (tin.at[1], hi(z, core), 2, z_dev(-1)),
        (tin.at[1], hi(z, core), 1, z_dev(1)),
        (tin.at[0], lo(z, core), 3, z_dev(-1)),
        (tin, full(z, core), 4, sib_dev),
    ):
        t_send(dst, which, dev, src)
    own_tok.wait()
    for c in range(EARLY):
        w_copy(c).wait()
    t_wait(full(z, other), 4)
    t_wait(lo(zm, core), 0)
    t_send(lo(zm, core), 5, z_dev(1))
    t_wait(hi(zp, core), 2)
    t_send(hi(zp, core), 6, z_dev(-1))
    early(z)
    t_wait(hi(zm, core), 1)
    t_send(full(zm, core), 7, sib_dev)
    t_wait(lo(zp, core), 3)
    t_send(full(zp, core), 8, sib_dev)
    t_wait(full(zm, other), 7)
    early(zm)
    t_wait(lo(zo, core), 5)
    t_send(lo(zo, core), 9, sib_dev)
    t_wait(hi(zo, core), 6)
    t_send(hi(zo, core), 10, sib_dev)
    t_wait(full(zp, other), 8)
    early(zp)
    t_wait(lo(zo, other), 9)
    t_wait(hi(zo, other), 10)
    early(zo)
    own_up.wait()


    def r_wait(region, kind, c, s, d):
        r_copy(region, region, kind, c, s, d, sib_dev).wait_recv()

    def s_wait(region, kind, c, s, d):
        r_copy(region, region, kind, c, s, d, sib_dev).wait_send()

    def cols_of(s):
        return slice(s * part, (s + 1) * part)

    def stage0(c):
        slot = lax.rem(c, 3)

        w_copy(c).wait()
        out = jnp.dot(
            tok[...].reshape(tokens_all, tok.shape[-1]), wv[c], preferred_element_type=F32
        )
        pf[lax.rem(c, 4)] = out.reshape(4, 4, slab, 2 * part)
        for s in (0, 1):
            m, cols = major[s], cols_of(s)
            for j in (0, 1):
                def piece(mm, k):
                    a, b = at(s, mm, k)
                    return pf[lax.rem(c, 4), a, b, :, cols].astype(BF16)

                snd1[c, s, 0, 0, j] = piece(mod4(m + 2), j)
                snd1[c, s, 0, 1, j] = piece(mod4(m + 1), 2 + j)
                snd1[c, s, 1, 0, j] = piece(mod4(m + 2), 2 + j)
                snd1[c, s, 1, 1, j] = piece(mod4(m - 1), j)
            for d in (0, 1):
                r_copy(snd1.at[c, s, d], rcv1.at[c, s, d], 0, c, s, d, major_dev[s](sign[d])).start()

    def stage1(c):
        slot = lax.rem(c, 3)
        for s in (0, 1):
            m, cols = major[s], cols_of(s)
            for d in (0, 1):
                r_wait(rcv1.at[c, s, d], 0, c, s, d)
                for j in (0, 1):
                    a, b = at(s, mod4(m + sign[d]), 2 * d + j)
                    sndc[c, s, d, j] = (
                        pf[lax.rem(c, 4), a, b, :, cols] + rcv1[c, s, d, 0, j].astype(F32)
                    ).astype(BF16)
                r_copy(sndc.at[c, s, d], rcvc.at[c, s, d], 1, c, s, d, major_dev[s](sign[d])).start()

    def stage2(c):
        slot = lax.rem(c, 3)
        for s in (0, 1):
            m, k, cols = major[s], minor[s], cols_of(s)
            for d in (0, 1):
                r_wait(rcvc.at[c, s, d], 1, c, s, d)
            for kk in range(4):
                a, b = at(s, m, kk)
                h, j = kk // 2, kk % 2
                s2[slot, s, kk] = (
                    pf[lax.rem(c, 4), a, b, :, cols]
                    + rcvc[c, s, h, j].astype(F32)
                    + rcv1[c, s, 1 - h, 1, j].astype(F32)
                )
            lo_c, hi_c = slice(0, half), slice(half, part)
            snd2[c, s, 0, 0] = s2[slot, s, mod4(k + 2), :, lo_c].astype(BF16)
            snd2[c, s, 0, 1] = s2[slot, s, mod4(k + 1), :, hi_c].astype(BF16)
            snd2[c, s, 1, 0] = s2[slot, s, mod4(k + 2), :, hi_c].astype(BF16)
            snd2[c, s, 1, 1] = s2[slot, s, mod4(k - 1), :, lo_c].astype(BF16)
            for d in (0, 1):
                r_copy(snd2.at[c, s, d], rcv2.at[c, s, d], 2, c, s, d, minor_dev[s](sign[d])).start()

    def stage3(c):
        slot = lax.rem(c, 3)
        for s in (0, 1):
            k = minor[s]
            for d in (0, 1):
                r_wait(rcv2.at[c, s, d], 2, c, s, d)
                cols = slice(d * half, (d + 1) * half)
                snd2c[c, s, d] = (
                    s2[slot, s, mod4(k + sign[d]), :, cols] + rcv2[c, s, d, 0].astype(F32)
                ).astype(BF16)
                r_copy(snd2c.at[c, s, d], rcv2c.at[c, s, d], 3, c, s, d, minor_dev[s](sign[d])).start()

    def stage4(c):
        slot = lax.rem(c, 3)
        for s in (0, 1):
            m, k = major[s], minor[s]
            a, b = at(s, m, k)
            for d in (0, 1):
                r_wait(rcv2c.at[c, s, d], 3, c, s, d)
            for h in (0, 1):
                cols = slice(h * half, (h + 1) * half)
                pre = (
                    s2[slot, s, k, :, cols]
                    + rcv2c[c, s, h].astype(F32)
                    + rcv2[c, s, 1 - h, 1].astype(F32)
                )
                at_col = pl.multiple_of(c * 2 * part + s * part + h * half, half)
                upstream = up[:, pl.ds(at_col, half)].astype(F32)
                g[c, s, a, b, :, cols] = (upstream * gelu_slope(pre)).astype(BF16)
            own = g.at[c, s, a, b]
            for d in (0, 1):
                r_copy(own, own, 4, c, s, d, minor_dev[s](sign[d])).start()

    def near(c, s, d):
        a, b = at(s, major[s], mod4(minor[s] - sign[d]))
        return g.at[c, s, a, b], g.at[c, s, a, b, :, pl.ds(d * half, half)]

    def far(c, s, d):
        a, b = at(s, major[s], mod4(minor[s] + 2))
        return g.at[c, s, a, b, :, pl.ds(d * half, half)]

    def stage5(c):
        for s in (0, 1):
            for d in (0, 1):
                whole, onward = near(c, s, d)
                r_wait(whole, 4, c, s, d)
                r_copy(onward, onward, 5, c, s, d, minor_dev[s](sign[d])).start()

    def line(c, s, m):
        return g.at[c, s, :, m] if s == 0 else g.at[c, s, m]

    def half_line(c, s, m, d):
        return g.at[c, s, pl.ds(2 * d, 2), m] if s == 0 else g.at[c, s, m, pl.ds(2 * d, 2)]

    def stage6(c):
        for s in (0, 1):
            for d in (0, 1):
                r_wait(far(c, s, d), 5, c, s, d)
            own = line(c, s, major[s])
            for d in (0, 1):
                r_copy(own, own, 6, c, s, d, major_dev[s](sign[d])).start()

    def stage7(c):
        for s in (0, 1):
            for d in (0, 1):
                m = mod4(major[s] - sign[d])
                r_wait(line(c, s, m), 6, c, s, d)
                onward = half_line(c, s, m, d)
                r_copy(onward, onward, 7, c, s, d, major_dev[s](sign[d])).start()

    def grad_of(c, s):
        return g[c, s].reshape(tokens_all, part)

    def land(c):
        for s in (0, 1):
            for d in (0, 1):
                r_wait(half_line(c, s, mod4(major[s] + 2), d), 7, c, s, d)

    def input_grad(c):
        total = None
        for s in (0, 1):
            term = lax.dot_general(
                grad_of(c, s), wv[c, :, cols_of(s)], (((1,), (1,)), ((), ())), preferred_element_type=F32
            )
            total = term if total is None else total + term
        giacc[...] += total.reshape(giacc.shape)

    def weight_grad(c):
        for s in (0, 1):
            gw_out[:, pl.ds(pl.multiple_of((c * 2 + s) * part, part), part)] = jnp.dot(
                tok_t[...], grad_of(c, s), preferred_element_type=F32
            ).astype(BF16)

    def settle(c):
        for s in (0, 1):
            m, k = major[s], minor[s]
            a, b = at(s, m, k)
            for d in (0, 1):
                s_wait(snd1.at[c, s, d], 0, c, s, d)
                s_wait(sndc.at[c, s, d], 1, c, s, d)
                s_wait(snd2.at[c, s, d], 2, c, s, d)
                s_wait(snd2c.at[c, s, d], 3, c, s, d)
                s_wait(g.at[c, s, a, b], 4, c, s, d)
                s_wait(near(c, s, d)[1], 5, c, s, d)
                s_wait(line(c, s, m), 6, c, s, d)
                s_wait(half_line(c, s, mod4(m - sign[d]), d), 7, c, s, d)

    def stage8(c):
        land(c)
        input_grad(c)

        weight_grad(c)
        settle(c)

    @pl.loop(1, n + 6)
    def _(i):
        for offset, stage in enumerate(
            (stage0, stage1, stage2, stage3, stage4, stage5, stage6, stage7)
        ):
            shift = offset if offset else -1
            start = EARLY if offset == 0 else 0

            @pl.when((i >= shift + start) & (i < n + shift))
            def _(shift=shift, stage=stage):
                stage(i - shift)

            if offset == 0:
                @pl.when(i == 3)
                def _():
                    for cp in sends:
                        cp.wait_send()
                    giacc[...] = jnp.zeros_like(giacc)
                    tok_t[...] = tok[...].reshape(tokens_all, tok.shape[-1]).T

        @pl.when((i >= 8))
        def _():
            stage8(i - 8)

    last = n - 1
    stage7(last)
    land(last - 1)
    input_grad(last - 1)
    land(last)

    def x_copy(src, dst, which, dev):
        return pltpu.make_async_remote_copy(
            src_ref=src, dst_ref=dst, send_sem=xsem_s.at[which], recv_sem=xsem_r.at[which],
            device_id=dev, device_id_type=MESH,
        )

    cross = []
    for which, zz in enumerate((zo, zp, zm, z)):
        total = None
        for s in (0, 1):
            term = lax.dot_general(
                g[last, s, zz].reshape(4 * slab, part), wv[last, :, cols_of(s)],
                (((1,), (1,)), ((), ())), preferred_element_type=F32,
            )
            total = term if total is None else total + term
        giacc[zz] += total.reshape(2, 2, slab, total.shape[-1])
        cp = x_copy(giacc.at[zz, other], gx.at[zz], which, sib_dev)
        cp.start()
        cross.append(cp)

    wire = zs1.dtype

    def both_cores(zz, h):
        return giacc[zz, core, h] + gx[zz, h]

    cross[0].wait()
    zs1[0, 0] = both_cores(zo, 0).astype(wire)
    zs1[1, 0] = both_cores(zo, 1).astype(wire)
    first = [
        [x_copy(zs1.at[d, ab], zr1.at[d, ab], 4 + 2 * ab + d, z_dev(sign[d])) for d in (0, 1)]
        for ab in (0, 1)
    ]
    first[0][0].start()
    first[0][1].start()
    cross[1].wait()
    zs1[0, 1] = both_cores(zp, 1).astype(wire)
    first[1][0].start()
    cross[2].wait()
    zs1[1, 1] = both_cores(zm, 0).astype(wire)
    first[1][1].start()
    weight_grad(last - 1)
    second = []
    for d in (0, 1):
        first[0][d].wait()
        zsc[d] = (both_cores(mod4(z + sign[d]), d) + zr1[d, 0].astype(F32)).astype(wire)
        cp = x_copy(zsc.at[d], zrc.at[d], 8 + d, z_dev(sign[d]))
        cp.start()
        second.append(cp)
    weight_grad(last)
    settle(last - 1)
    settle(last)
    cross[3].wait()
    for d in (0, 1):
        first[1][d].wait()
    for d in (0, 1):
        second[d].wait()
        gi_out[pl.ds(d * slab, slab), :] = (
            both_cores(z, d) + zrc[d].astype(F32) + zr1[1 - d, 1].astype(F32)
        ).astype(BF16)


def flush(gi, gw, gi_out, gw_out, sem):
    step = gw.shape[0] // FLUSHES
    copies = [pltpu.make_async_copy(gi, gi_out, sem.at[FLUSHES])]
    for j in range(FLUSHES):
        rows = pl.ds(j * step, step)
        copies.append(pltpu.make_async_copy(gw.at[rows], gw_out.at[rows], sem.at[j]))
    for cp in copies:
        cp.start()
    for cp in copies:
        cp.wait()


def local(tokens, weight, upstream):
    rows, depth = tokens.shape
    width = weight.shape[1]
    slab = upstream.shape[0]
    n = N_CHUNKS
    part = width // (2 * n)
    half = part // 2
    wire = BF16
    vmem, dma = pltpu.VMEM, pltpu.SemaphoreType.DMA
    scratch = [
        vmem((slab, width), BF16),
        vmem((4, 2, 2, slab, depth), BF16),
        vmem((depth, 16 * slab), BF16),
        vmem((n, depth, 2 * part), BF16),
        vmem((4, 4, 4, slab, 2 * part), F32),
        vmem((n, 2, 2, 2, 2, slab, part), BF16),
        vmem((n, 2, 2, 2, 2, slab, part), BF16),
        vmem((n, 2, 2, 2, slab, part), BF16),
        vmem((n, 2, 2, 2, slab, part), BF16),
        vmem((3, 2, 4, slab, part), F32),
        vmem((n, 2, 2, 2, slab, half), BF16),
        vmem((n, 2, 2, 2, slab, half), BF16),
        vmem((n, 2, 2, slab, half), BF16),
        vmem((n, 2, 2, slab, half), BF16),
        vmem((n, 2, 4, 4, slab, part), BF16),
        vmem((4, 2, 2, slab, depth), F32),
        vmem((4, 2, slab, depth), F32),
        vmem((2, 2, slab, depth), wire),
        vmem((2, 2, slab, depth), wire),
        vmem((2, slab, depth), wire),
        vmem((2, slab, depth), wire),
        dma((n, 2, 8, 2)),
        dma((n, 2, 8, 2)),
        dma((11,)),
        dma((11,)),
        dma((10,)),
        dma((10,)),
        dma((n,)),
        dma((2,)),
    ]
    gi, gw = pl.pallas_call(
        functools.partial(kernel, n, part, slab),
        out_shape=(
            pltpu.VMEM((rows, depth), BF16),
            pltpu.VMEM((depth, width), BF16),
        ),
        in_specs=[
            pl.BlockSpec(memory_space=pl.ANY),
            pl.BlockSpec(memory_space=pl.ANY),
            pl.BlockSpec(memory_space=pl.ANY),
        ],
        out_specs=(
            pl.BlockSpec(memory_space=pltpu.VMEM),
            pl.BlockSpec(memory_space=pltpu.VMEM),
        ),
        scratch_shapes=scratch,
        compiler_params=pltpu.CompilerParams(
            collective_id=0, has_side_effects=True, vmem_limit_bytes=56 * 1024 * 1024 + 512 * 1024
        ),
        cost_estimate=pl.CostEstimate(
            flops=6 * 16 * slab * depth * width, bytes_accessed=4 * depth * width, transcendentals=slab * width
        ),
    )(tokens.reshape(2, rows // 2, depth), weight, upstream)

    return pl.pallas_call(
        flush,
        out_shape=(
            jax.ShapeDtypeStruct((rows, depth), BF16),
            jax.ShapeDtypeStruct((depth, width), BF16),
        ),
        in_specs=[pl.BlockSpec(memory_space=pltpu.VMEM)] * 2,
        out_specs=(pl.BlockSpec(memory_space=pl.ANY),) * 2,
        scratch_shapes=[dma((FLUSHES + 1,))],
        compiler_params=pltpu.CompilerParams(vmem_limit_bytes=1024 * 1024),
    )(pltpu.with_memory_space_constraint(gi, pltpu.VMEM), pltpu.with_memory_space_constraint(gw, pltpu.VMEM))


def solution(mesh):
    spec = PartitionSpec
    return jax.shard_map(
        local,
        mesh=mesh,
        in_specs=(spec("row", "col"), spec("col", "row"), spec("col", "row")),
        out_specs=(spec("row", "col"), spec("col", "row")),
        check_vma=False,
    )
```

```python
import functools

import jax
import jax.numpy as jnp
from jax import lax
from jax.experimental import pallas as pl
from jax.experimental.pallas import tpu as pltpu
from jax.sharding import PartitionSpec

N_CHUNKS = 5
EARLY = 2
FLUSHES = 8
BF16 = jnp.bfloat16
F32 = jnp.float32
MESH = pl.DeviceIdType.MESH


def gelu_slope(value):
    coeff = 0.7978845608028654
    inner = coeff * (value + 0.044715 * value * value * value)
    tanh_value = jnp.tanh(inner)
    return 0.5 * (1.0 + tanh_value) + 0.5 * value * (1.0 - tanh_value * tanh_value) * coeff * (
        1.0 + 3.0 * 0.044715 * value * value
    )


def mod4(value):
    return lax.rem(value + 4, 4)


def kernel(
    n, part, slab,
    tin, w_hbm, up_hbm, gi_out, gw_out,
    up, tok, tok_t, wv, pf, snd1, rcv1, sndc, rcvc, s2, snd2, rcv2, snd2c, rcv2c, g, giacc,
    gx, zs1, zr1, zsc, zrc,
    ssem, rsem, tsem_s, tsem_r, xsem_s, xsem_r, wsem, lsem,
):
    row, col = lax.axis_index("row"), lax.axis_index("col")
    z, core = lax.div(row, 2), lax.rem(row, 2)
    y, x = lax.div(col, 4), lax.rem(col, 4)
    half = part // 2

    def x_dev(d):
        return {"col": y * 4 + mod4(x + d)}

    def y_dev(d):
        return {"col": mod4(y + d) * 4 + x}

    def z_dev(d):
        return {"row": mod4(z + d) * 2 + core}

    sib_dev = {"row": z * 2 + (1 - core)}
    sign = (1, -1)
    major, minor = (x, y), (y, x)
    major_dev, minor_dev = (x_dev, y_dev), (y_dev, x_dev)

    def at(s, m, k):
        return (k, m) if s == 0 else (m, k)

    def w_copy(c):
        return pltpu.make_async_copy(
            w_hbm.at[:, pl.ds(pl.multiple_of(c * 2 * part, 2 * part), 2 * part)], wv.at[c], wsem.at[c]
        )

    barrier = pltpu.get_barrier_semaphore()
    for dev in (x_dev(1), x_dev(-1), y_dev(1), y_dev(-1), z_dev(1), z_dev(-1), sib_dev):
        pl.semaphore_signal(barrier, inc=1, device_id=dev, device_id_type=MESH)
    own_tok = pltpu.make_async_copy(tin, tok.at[z, core], lsem.at[0])
    own_tok.start()
    for c in range(n):
        w_copy(c).start()
    own_up = pltpu.make_async_copy(up_hbm, up, lsem.at[1])
    own_up.start()
    pl.semaphore_wait(barrier, 7)

    def t_copy(region, which, dev, src=None):
        return pltpu.make_async_remote_copy(
            src_ref=region if src is None else src, dst_ref=region, send_sem=tsem_s.at[which], recv_sem=tsem_r.at[which],
            device_id=dev, device_id_type=MESH,
        )

    def full(zz, cc):
        return tok.at[zz, cc]

    def lo(zz, cc):
        return tok.at[zz, cc, 0]

    def hi(zz, cc):
        return tok.at[zz, cc, 1]

    zm, zp, zo = mod4(z - 1), mod4(z + 1), mod4(z + 2)
    other = 1 - core
    tokens_all = 16 * slab
    sends = []

    def t_send(region, which, dev, src=None):
        cp = t_copy(region, which, dev, src)
        cp.start()
        sends.append(cp)

    def t_wait(region, which):
        t_copy(region, which, sib_dev).wait_recv()

    def r_copy(src, dst, kind, c, s, d, dev):
        return pltpu.make_async_remote_copy(
            src_ref=src, dst_ref=dst, send_sem=ssem.at[c, s, kind, d], recv_sem=rsem.at[c, s, kind, d],
            device_id=dev, device_id_type=MESH,
        )

    def early(zz):
        rows = tok[zz].reshape(4 * slab, tok.shape[-1])
        h, j = lax.div(zz, 2), lax.rem(zz, 2)
        q = mod4(zz - y)
        for c in range(EARLY):
            pf[c, zz] = jnp.dot(rows, wv[c], preferred_element_type=F32).reshape(4, slab, 2 * part)
            for d in (0, 1):
                ab = h if d == 0 else 1 - h
                owner = mod4(x + 2 - h) if d == 0 else mod4(x + 3 - h)
                piece = snd1.at[c, 0, d, ab, j]
                piece[...] = pf[c, zz, owner, :, :part].astype(BF16)
                r_copy(piece, rcv1.at[c, 0, d, ab, j], 0, c, 0, d, x_dev(sign[d])).start()

            def unit(d, ab, k0, c=c):
                snd1[c, 1, d, ab] = pf[c, zz, k0:k0 + 2, :, part:].astype(BF16)
                r_copy(snd1.at[c, 1, d, ab], rcv1.at[c, 1, d, ab], 0, c, 1, d, y_dev(sign[d])).start()

            @pl.when(q == 1)
            def _():
                unit(0, 1, 2)

            @pl.when(q == 2)
            def _():
                unit(0, 0, 0)
                unit(1, 0, 2)

            @pl.when(q == 3)
            def _():
                unit(1, 1, 0)

    for src, dst, which, dev in (
        (tin.at[0], lo(z, core), 0, z_dev(1)),
        (tin.at[1], hi(z, core), 2, z_dev(-1)),
        (tin.at[1], hi(z, core), 1, z_dev(1)),
        (tin.at[0], lo(z, core), 3, z_dev(-1)),
        (tin, full(z, core), 4, sib_dev),
    ):
        t_send(dst, which, dev, src)
    own_tok.wait()
    for c in range(EARLY):
        w_copy(c).wait()
    t_wait(full(z, other), 4)
    early(z)
    t_wait(lo(zm, core), 0)
    t_send(lo(zm, core), 5, z_dev(1))
    t_wait(hi(zp, core), 2)
    t_send(hi(zp, core), 6, z_dev(-1))
    t_wait(hi(zm, core), 1)
    t_send(full(zm, core), 7, sib_dev)
    t_wait(lo(zp, core), 3)
    t_send(full(zp, core), 8, sib_dev)
    t_wait(full(zm, other), 7)
    early(zm)
    t_wait(lo(zo, core), 5)
    t_send(lo(zo, core), 9, sib_dev)
    t_wait(hi(zo, core), 6)
    t_send(hi(zo, core), 10, sib_dev)
    t_wait(full(zp, other), 8)
    early(zp)
    t_wait(lo(zo, other), 9)
    t_wait(hi(zo, other), 10)
    early(zo)
    own_up.wait()


    def r_wait(region, kind, c, s, d):
        r_copy(region, region, kind, c, s, d, sib_dev).wait_recv()

    def s_wait(region, kind, c, s, d):
        r_copy(region, region, kind, c, s, d, sib_dev).wait_send()

    def cols_of(s):
        return slice(s * part, (s + 1) * part)

    def stage0(c):
        slot = lax.rem(c, 3)

        w_copy(c).wait()
        out = jnp.dot(
            tok[...].reshape(tokens_all, tok.shape[-1]), wv[c], preferred_element_type=F32
        )
        pf[lax.rem(c, 4)] = out.reshape(4, 4, slab, 2 * part)
        for s in (0, 1):
            m, cols = major[s], cols_of(s)
            for j in (0, 1):
                def piece(mm, k):
                    a, b = at(s, mm, k)
                    return pf[lax.rem(c, 4), a, b, :, cols].astype(BF16)

                snd1[c, s, 0, 0, j] = piece(mod4(m + 2), j)
                snd1[c, s, 0, 1, j] = piece(mod4(m + 1), 2 + j)
                snd1[c, s, 1, 0, j] = piece(mod4(m + 2), 2 + j)
                snd1[c, s, 1, 1, j] = piece(mod4(m - 1), j)
            for d in (0, 1):
                r_copy(snd1.at[c, s, d], rcv1.at[c, s, d], 0, c, s, d, major_dev[s](sign[d])).start()

    def stage1(c):
        slot = lax.rem(c, 3)
        for s in (0, 1):
            m, cols = major[s], cols_of(s)
            for d in (0, 1):
                r_wait(rcv1.at[c, s, d], 0, c, s, d)
                for j in (0, 1):
                    a, b = at(s, mod4(m + sign[d]), 2 * d + j)
                    sndc[c, s, d, j] = (
                        pf[lax.rem(c, 4), a, b, :, cols] + rcv1[c, s, d, 0, j].astype(F32)
                    ).astype(BF16)
                r_copy(sndc.at[c, s, d], rcvc.at[c, s, d], 1, c, s, d, major_dev[s](sign[d])).start()

    def stage2(c):
        slot = lax.rem(c, 3)
        for s in (0, 1):
            m, k, cols = major[s], minor[s], cols_of(s)
            for d in (0, 1):
                r_wait(rcvc.at[c, s, d], 1, c, s, d)
            for kk in range(4):
                a, b = at(s, m, kk)
                h, j = kk // 2, kk % 2
                s2[slot, s, kk] = (
                    pf[lax.rem(c, 4), a, b, :, cols]
                    + rcvc[c, s, h, j].astype(F32)
                    + rcv1[c, s, 1 - h, 1, j].astype(F32)
                )
            lo_c, hi_c = slice(0, half), slice(half, part)
            snd2[c, s, 0, 0] = s2[slot, s, mod4(k + 2), :, lo_c].astype(BF16)
            snd2[c, s, 0, 1] = s2[slot, s, mod4(k + 1), :, hi_c].astype(BF16)
            snd2[c, s, 1, 0] = s2[slot, s, mod4(k + 2), :, hi_c].astype(BF16)
            snd2[c, s, 1, 1] = s2[slot, s, mod4(k - 1), :, lo_c].astype(BF16)
            for d in (0, 1):
                r_copy(snd2.at[c, s, d], rcv2.at[c, s, d], 2, c, s, d, minor_dev[s](sign[d])).start()

    def stage3(c):
        slot = lax.rem(c, 3)
        for s in (0, 1):
            k = minor[s]
            for d in (0, 1):
                r_wait(rcv2.at[c, s, d], 2, c, s, d)
                cols = slice(d * half, (d + 1) * half)
                snd2c[c, s, d] = (
                    s2[slot, s, mod4(k + sign[d]), :, cols] + rcv2[c, s, d, 0].astype(F32)
                ).astype(BF16)
                r_copy(snd2c.at[c, s, d], rcv2c.at[c, s, d], 3, c, s, d, minor_dev[s](sign[d])).start()

    def stage4(c):
        slot = lax.rem(c, 3)
        for s in (0, 1):
            m, k = major[s], minor[s]
            a, b = at(s, m, k)
            for d in (0, 1):
                r_wait(rcv2c.at[c, s, d], 3, c, s, d)
            for h in (0, 1):
                cols = slice(h * half, (h + 1) * half)
                pre = (
                    s2[slot, s, k, :, cols]
                    + rcv2c[c, s, h].astype(F32)
                    + rcv2[c, s, 1 - h, 1].astype(F32)
                )
                at_col = pl.multiple_of(c * 2 * part + s * part + h * half, half)
                upstream = up[:, pl.ds(at_col, half)].astype(F32)
                g[c, s, a, b, :, cols] = (upstream * gelu_slope(pre)).astype(BF16)
            own = g.at[c, s, a, b]
            for d in (0, 1):
                r_copy(own, own, 4, c, s, d, minor_dev[s](sign[d])).start()

    def near(c, s, d):
        a, b = at(s, major[s], mod4(minor[s] - sign[d]))
        return g.at[c, s, a, b], g.at[c, s, a, b, :, pl.ds(d * half, half)]

    def far(c, s, d):
        a, b = at(s, major[s], mod4(minor[s] + 2))
        return g.at[c, s, a, b, :, pl.ds(d * half, half)]

    def stage5(c):
        for s in (0, 1):
            for d in (0, 1):
                whole, onward = near(c, s, d)
                r_wait(whole, 4, c, s, d)
                r_copy(onward, onward, 5, c, s, d, minor_dev[s](sign[d])).start()

    def line(c, s, m):
        return g.at[c, s, :, m] if s == 0 else g.at[c, s, m]

    def half_line(c, s, m, d):
        return g.at[c, s, pl.ds(2 * d, 2), m] if s == 0 else g.at[c, s, m, pl.ds(2 * d, 2)]

    def stage6(c):
        for s in (0, 1):
            for d in (0, 1):
                r_wait(far(c, s, d), 5, c, s, d)
            for turn, kind in ((0, 6), (1, 8)):
                for d in (0, 1):
                    own = half_line(c, s, major[s], d if turn == 0 else 1 - d)
                    r_copy(own, own, kind, c, s, d, major_dev[s](sign[d])).start()

    def stage7(c):
        for s in (0, 1):
            for d in (0, 1):
                m = mod4(major[s] - sign[d])
                onward = half_line(c, s, m, d)
                r_wait(onward, 6, c, s, d)
                r_copy(onward, onward, 7, c, s, d, major_dev[s](sign[d])).start()

    def grad_of(c, s):
        return g[c, s].reshape(tokens_all, part)

    def land(c):
        for s in (0, 1):
            for d in (0, 1):
                r_wait(half_line(c, s, mod4(major[s] - sign[d]), 1 - d), 8, c, s, d)
                r_wait(half_line(c, s, mod4(major[s] + 2), d), 7, c, s, d)

    def input_grad(c):
        total = None
        for s in (0, 1):
            term = lax.dot_general(
                grad_of(c, s), wv[c, :, cols_of(s)], (((1,), (1,)), ((), ())), preferred_element_type=F32
            )
            total = term if total is None else total + term
        giacc[...] += total.reshape(giacc.shape)

    def weight_grad(c):
        for s in (0, 1):
            gw_out[:, pl.ds(pl.multiple_of((c * 2 + s) * part, part), part)] = jnp.dot(
                tok_t[...], grad_of(c, s), preferred_element_type=F32
            ).astype(BF16)

    def settle(c):
        for s in (0, 1):
            m, k = major[s], minor[s]
            a, b = at(s, m, k)
            for d in (0, 1):
                s_wait(snd1.at[c, s, d], 0, c, s, d)
                s_wait(sndc.at[c, s, d], 1, c, s, d)
                s_wait(snd2.at[c, s, d], 2, c, s, d)
                s_wait(snd2c.at[c, s, d], 3, c, s, d)
                s_wait(g.at[c, s, a, b], 4, c, s, d)
                s_wait(near(c, s, d)[1], 5, c, s, d)
                s_wait(half_line(c, s, m, d), 6, c, s, d)
                s_wait(half_line(c, s, m, 1 - d), 8, c, s, d)
                s_wait(half_line(c, s, mod4(m - sign[d]), d), 7, c, s, d)

    def stage8(c):
        land(c)
        input_grad(c)

        weight_grad(c)
        settle(c)

    @pl.loop(1, n + 6)
    def _(i):
        for offset, stage in enumerate(
            (stage0, stage1, stage2, stage3, stage4, stage5, stage6, stage7)
        ):
            shift = offset if offset else -1
            start = EARLY if offset == 0 else 0

            @pl.when((i >= shift + start) & (i < n + shift))
            def _(shift=shift, stage=stage):
                stage(i - shift)

            if offset == 0:
                @pl.when(i == 3)
                def _():
                    for cp in sends:
                        cp.wait_send()
                    giacc[...] = jnp.zeros_like(giacc)
                    tok_t[...] = tok[...].reshape(tokens_all, tok.shape[-1]).T

        @pl.when((i >= 8))
        def _():
            stage8(i - 8)

    last = n - 1
    stage7(last)
    land(last - 1)
    input_grad(last - 1)
    land(last)

    def x_copy(src, dst, which, dev):
        return pltpu.make_async_remote_copy(
            src_ref=src, dst_ref=dst, send_sem=xsem_s.at[which], recv_sem=xsem_r.at[which],
            device_id=dev, device_id_type=MESH,
        )

    cross = []
    for which, zz in enumerate((zo, zp, zm, z)):
        total = None
        for s in (0, 1):
            term = lax.dot_general(
                g[last, s, zz].reshape(4 * slab, part), wv[last, :, cols_of(s)],
                (((1,), (1,)), ((), ())), preferred_element_type=F32,
            )
            total = term if total is None else total + term
        giacc[zz] += total.reshape(2, 2, slab, total.shape[-1])
        cp = x_copy(giacc.at[zz, other], gx.at[zz], which, sib_dev)
        cp.start()
        cross.append(cp)

    wire = zs1.dtype

    def both_cores(zz, h):
        return giacc[zz, core, h] + gx[zz, h]

    cross[0].wait()
    zs1[0, 0] = both_cores(zo, 0).astype(wire)
    zs1[1, 0] = both_cores(zo, 1).astype(wire)
    first = [
        [x_copy(zs1.at[d, ab], zr1.at[d, ab], 4 + 2 * ab + d, z_dev(sign[d])) for d in (0, 1)]
        for ab in (0, 1)
    ]
    first[0][0].start()
    first[0][1].start()
    cross[1].wait()
    zs1[0, 1] = both_cores(zp, 1).astype(wire)
    first[1][0].start()
    cross[2].wait()
    zs1[1, 1] = both_cores(zm, 0).astype(wire)
    first[1][1].start()
    weight_grad(last - 1)
    second = []
    for d in (0, 1):
        first[0][d].wait()
        zsc[d] = (both_cores(mod4(z + sign[d]), d) + zr1[d, 0].astype(F32)).astype(wire)
        cp = x_copy(zsc.at[d], zrc.at[d], 8 + d, z_dev(sign[d]))
        cp.start()
        second.append(cp)
    weight_grad(last)
    settle(last - 1)
    settle(last)
    cross[3].wait()
    for d in (0, 1):
        first[1][d].wait()
    for d in (0, 1):
        second[d].wait()
        gi_out[pl.ds(d * slab, slab), :] = (
            both_cores(z, d) + zrc[d].astype(F32) + zr1[1 - d, 1].astype(F32)
        ).astype(BF16)


def flush(gi, gw, gi_out, gw_out, sem):
    step = gw.shape[0] // FLUSHES
    copies = [pltpu.make_async_copy(gi, gi_out, sem.at[FLUSHES])]
    for j in range(FLUSHES):
        rows = pl.ds(j * step, step)
        copies.append(pltpu.make_async_copy(gw.at[rows], gw_out.at[rows], sem.at[j]))
    for cp in copies:
        cp.start()
    for cp in copies:
        cp.wait()


def local(tokens, weight, upstream):
    rows, depth = tokens.shape
    width = weight.shape[1]
    slab = upstream.shape[0]
    n = N_CHUNKS
    part = width // (2 * n)
    half = part // 2
    wire = BF16
    vmem, dma = pltpu.VMEM, pltpu.SemaphoreType.DMA
    scratch = [
        vmem((slab, width), BF16),
        vmem((4, 2, 2, slab, depth), BF16),
        vmem((depth, 16 * slab), BF16),
        vmem((n, depth, 2 * part), BF16),
        vmem((4, 4, 4, slab, 2 * part), F32),
        vmem((n, 2, 2, 2, 2, slab, part), BF16),
        vmem((n, 2, 2, 2, 2, slab, part), BF16),
        vmem((n, 2, 2, 2, slab, part), BF16),
        vmem((n, 2, 2, 2, slab, part), BF16),
        vmem((3, 2, 4, slab, part), F32),
        vmem((n, 2, 2, 2, slab, half), BF16),
        vmem((n, 2, 2, 2, slab, half), BF16),
        vmem((n, 2, 2, slab, half), BF16),
        vmem((n, 2, 2, slab, half), BF16),
        vmem((n, 2, 4, 4, slab, part), BF16),
        vmem((4, 2, 2, slab, depth), F32),
        vmem((4, 2, slab, depth), F32),
        vmem((2, 2, slab, depth), wire),
        vmem((2, 2, slab, depth), wire),
        vmem((2, slab, depth), wire),
        vmem((2, slab, depth), wire),
        dma((n, 2, 9, 2)),
        dma((n, 2, 9, 2)),
        dma((11,)),
        dma((11,)),
        dma((10,)),
        dma((10,)),
        dma((n,)),
        dma((2,)),
    ]
    gi, gw = pl.pallas_call(
        functools.partial(kernel, n, part, slab),
        out_shape=(
            pltpu.VMEM((rows, depth), BF16),
            pltpu.VMEM((depth, width), BF16),
        ),
        in_specs=[
            pl.BlockSpec(memory_space=pl.ANY),
            pl.BlockSpec(memory_space=pl.ANY),
            pl.BlockSpec(memory_space=pl.ANY),
        ],
        out_specs=(
            pl.BlockSpec(memory_space=pltpu.VMEM),
            pl.BlockSpec(memory_space=pltpu.VMEM),
        ),
        scratch_shapes=scratch,
        compiler_params=pltpu.CompilerParams(
            collective_id=0, has_side_effects=True, vmem_limit_bytes=56 * 1024 * 1024 + 512 * 1024
        ),
        cost_estimate=pl.CostEstimate(
            flops=6 * 16 * slab * depth * width, bytes_accessed=4 * depth * width, transcendentals=slab * width
        ),
    )(tokens.reshape(2, rows // 2, depth), weight, upstream)

    return pl.pallas_call(
        flush,
        out_shape=(
            jax.ShapeDtypeStruct((rows, depth), BF16),
            jax.ShapeDtypeStruct((depth, width), BF16),
        ),
        in_specs=[pl.BlockSpec(memory_space=pltpu.VMEM)] * 2,
        out_specs=(pl.BlockSpec(memory_space=pl.ANY),) * 2,
        scratch_shapes=[dma((FLUSHES + 1,))],
        compiler_params=pltpu.CompilerParams(vmem_limit_bytes=1024 * 1024),
    )(pltpu.with_memory_space_constraint(gi, pltpu.VMEM), pltpu.with_memory_space_constraint(gw, pltpu.VMEM))


def solution(mesh):
    spec = PartitionSpec
    return jax.shard_map(
        local,
        mesh=mesh,
        in_specs=(spec("row", "col"), spec("col", "row"), spec("col", "row")),
        out_specs=(spec("row", "col"), spec("col", "row")),
        check_vma=False,
    )
```
